128 devices in a mesh: occ: 4 (over y_hi, core), aux: 32 (over x, z, y_lo).
Axes of the slice: x: 4, y: 4 (y_hi: 2, y_lo: 2; y = y_hi * 2 + y_lo), z: 4, core: 2. Of those that a mesh axis runs over, the one named last changes fastest.
Arguments:
- three_index: bfloat16 [12000, 6, 1920], P('aux'), may hold values from -0.47851562 to 0.47851562
- occ_energy: float32 [6], replicated, may hold values from -1.5 to -0.3
- vir_energy: float32 [1920], replicated, may hold values from 0.25 to 2.95
- batch_table: int32 [6], replicated, may hold values from 0 to 5, each once
- orbital_order: int32 [6], replicated, may hold values from 0 to 5, each once
- occ_pair_int: bfloat16 [2, 2, 12000], P(None, None, 'aux'), may hold values from -0.03881836 to 0.03881836
- half_ao: bfloat16 [2, 12000, 4000], P(None, 'aux'), may hold values from -9.536743e-06 to 9.536743e-06
- vir_coeff: bfloat16 [4000, 1920], P('aux', 'occ'), may hold values from -0.09375 to 0.09375
Outputs:
- gamma: bfloat16 [12000, 2, 1920], P('aux', None, 'occ')
- orbital_gradient: float32 [2, 1920], P(None, ('occ', 'aux'))
The draws below stay inside these ranges and needn't reach their ends.
Inputs may be any that keep to these rules, and one draw needn't show every extreme that they name: `batch_table`: a permutation of 0 to 5; its first 4 entries are the partner orbitals of the window. `orbital_order`: a permutation of 0 to 5; its first 2 entries are the orbitals whose amplitudes are formed.
All inputs are finite; a program needn't handle non-finite values.
Results may differ from the reference program's by a relative error of at most 0.019.
Values may be sent and summed in bfloat16 or wider, within the bound.
No kernel may reach another device: no remote copies, remote signals or barrier semaphores. Data moves between devices by JAX's collectives and lax.ppermute only.
A program may use at most 128 MiB of HBM per device.

```python
import jax
import jax.numpy as jnp
from jax import lax

NAUX = 12000
NVIR = 1920
NBF = 4000
NI = 2
NPART_DEV = 1
NOCC_B = 6
N_OCC = 4
N_AUX = 32


def draw_vir_energy(key, part):
    increments = jax.random.uniform(key, (NVIR,), jnp.float32, 0.5, 1.5)
    return 0.25 + 2.7 * jnp.cumsum(increments) / jnp.sum(increments)


def block_levels(key, dims, shards, least, top_value):
    loudness, own = 1.0, jax.random.fold_in(key, 6)
    for position, shards_of in shards:
        draws = jnp.exp(jax.random.uniform(jax.random.fold_in(own, position), (shards_of,), jnp.float32, least / len(shards), top_value / len(shards)))
        loudness = loudness * jnp.repeat(draws, dims[position] // shards_of).reshape([-1 if axis == position else 1 for axis in range(len(dims))])
    return loudness


def gaussian(rng, extent, width, reach, cuts=(), kind=jnp.bfloat16):
    drawn = jax.random.normal(rng, extent, jnp.float32) * width
    if len(cuts) > 0:
        drawn = block_levels(rng, extent, cuts, -0.22, 0.18) * drawn
    return jnp.clip(drawn, min=-reach, max=reach).astype(kind)


def setup_inputs(seed: int = 0) -> dict:
    splits = jax.random.split(jax.random.key(seed), 9)
    three_index = gaussian(splits[0], (NAUX, NOCC_B, NVIR), 0.08, 0.47851562, ((0, 32),))
    occ_energy = jnp.clip(jax.random.uniform(splits[1], (NOCC_B,), jnp.float32, -1.5, -0.3), -1.5, -0.3)
    vir_energy = draw_vir_energy(jax.random.fold_in(splits[8], 71), 0)
    batch_table = jax.random.permutation(splits[3], NOCC_B).astype(jnp.int32)
    orbital_order = jax.random.permutation(splits[4], NOCC_B).astype(jnp.int32)
    occ_pair_int = gaussian(splits[5], (NI, NI, NAUX), 0.0065, 0.03881836, ((2, 32),))
    half_ao = gaussian(splits[6], (NI, NAUX, NBF), (456976 * NVIR ** 4 * (N_OCC * NPART_DEV) ** 2 * 2 * NAUX ** 3 // (9 * 10 ** 20) + 1) ** -0.5, 9.5367431640625e-06, ((1, 32),))
    vir_coeff = gaussian(splits[7], (NBF, NVIR), NBF ** -0.5, 0.09375, ((0, 32), (1, 4)))
    return {"three_index": three_index, "occ_energy": occ_energy, "vir_energy": vir_energy, "batch_table": batch_table, "orbital_order": orbital_order, "occ_pair_int": occ_pair_int, "half_ao": half_ao, "vir_coeff": vir_coeff}


def reference(three_index, occ_energy, vir_energy, batch_table, orbital_order, occ_pair_int, half_ao, vir_coeff):
    own_orbits = orbital_order[:NI]
    partner_orbits = batch_table[:N_OCC * NPART_DEV]
    left_block = jnp.take(three_index, own_orbits, axis=1).astype(jnp.float32)
    right_block = jnp.take(three_index, partner_orbits, axis=1).astype(jnp.float32)
    block_size = NAUX // N_AUX
    left_blocks = left_block.reshape(N_AUX, block_size, NI, NVIR)
    right_blocks = right_block.reshape(N_AUX, block_size, N_OCC * NPART_DEV, NVIR)

    def add_block(running, blocks_pair):
        partial_pairs = jnp.einsum("qsa,qkb->askb", blocks_pair[0], blocks_pair[1])
        rounded = lax.optimization_barrier(partial_pairs.astype(jnp.bfloat16))
        return running + rounded.astype(jnp.float32), None

    start_sum = jnp.zeros((NVIR, NI, N_OCC * NPART_DEV, NVIR), jnp.float32)
    pair_sum, _ = lax.scan(add_block, start_sum, (left_blocks, right_blocks))
    denominator = (vir_energy[:, None, None, None] + vir_energy[None, None, None, :]
                   - jnp.take(occ_energy, own_orbits)[None, :, None, None]
                   - jnp.take(occ_energy, partner_orbits)[None, None, :, None])
    amplitudes = (-pair_sum / denominator).astype(jnp.bfloat16)
    amps_wide = amplitudes.astype(jnp.float32)
    gamma_out = jnp.einsum("askb,qkb->qsa", amps_wide, right_block).astype(jnp.bfloat16)
    density = -jnp.einsum("askb,atkb->st", amps_wide, amps_wide)
    pair_int = occ_pair_int.astype(jnp.float32)
    coulomb = jnp.einsum("stq,st->q", pair_int, density, precision=lax.Precision.HIGHEST)
    exchange = jnp.einsum("suq,tu->stq", pair_int, density, precision=lax.Precision.HIGHEST)
    identity = jnp.eye(NI, dtype=jnp.float32)
    coefficient = (2.0 * identity[:, :, None] * coulomb[None, None, :] - exchange).astype(jnp.bfloat16)
    fock = jnp.dot(coefficient.reshape(NI, NI * NAUX), half_ao.reshape(NI * NAUX, NBF), preferred_element_type=jnp.float32)
    occ_side = -jnp.einsum("usq,qua->sa", pair_int, gamma_out.astype(jnp.float32))
    vir_side = jnp.dot(fock, vir_coeff.astype(jnp.float32), precision=lax.Precision.HIGHEST)
    return gamma_out, occ_side + vir_side
```

```python
import jax
import jax.numpy as jnp
from jax import lax
from jax.sharding import Mesh
from jax.sharding import PartitionSpec as P

NI = 2
KH = 2
ROWS = 30
PAD = 32
AUX = ("x", "z", "yl")
OCC_AUX = ("yh", "core", "x", "z", "yl")
F32 = jnp.float32
BF16 = jnp.bfloat16


def ring(n, d):
    return [(i, (i + d) % n) for i in range(n)]


def up(v, axis):
    return lax.ppermute(v, axis, ring(4, 1))


def down(v, axis):
    return lax.ppermute(v, axis, ring(4, -1))


def dot(a, b, dims):
    return lax.dot_general(a, b, (dims, ((), ())), preferred_element_type=F32)


def ring_sum(v, axis):
    lo2, hi2 = v[2]
    got_up = up(lo2.astype(BF16), axis)
    got_down = down(hi2.astype(BF16), axis)
    one = jnp.concatenate([v[1][0] + got_up.astype(F32), v[1][1]]).astype(BF16)
    three = jnp.concatenate([v[3][0], v[3][1] + got_down.astype(F32)]).astype(BF16)
    from_below = up(one, axis)
    from_above = down(three, axis)
    own = jnp.concatenate([v[0][0], v[0][1]])
    return own + from_below.astype(F32) + from_above.astype(F32)


def ring_gather(v, axis):
    below = up(v, axis)
    above = down(v, axis)
    half = v.shape[0] // 2
    lo = up(below[:half], axis)
    hi = down(above[half:], axis)
    return [v, above, jnp.concatenate([lo, hi]), below]


def local(
    three_index,
    occ_energy,
    vir_energy,
    batch_table,
    orbital_order,
    occ_pair_int,
    half_ao,
    vir_coeff,
):
    nq, _, nvirt = three_index.shape
    yh, core, x, z, yl = (lax.axis_index(a) for a in OCC_AUX)
    own_a = (yh * 2 + core) * (nvirt // 4)
    by_orbital = jnp.transpose(three_index, (1, 0, 2))

    def orbital(i):
        return lax.dynamic_index_in_dim(by_orbital, i, 0, keepdims=False)

    def partner_orbital(half, k):
        return lax.dynamic_index_in_dim(batch_table, half * KH + k, 0, keepdims=False)

    pairs = []
    for h in range(2):
        for c in range(2):
            for t in range(2):
                src = h * 4 + c * 2 + t
                dst = (h if c == 0 else 1 - h) * 4 + c * 2 + (1 - t)
                pairs.append((src, dst))
    swap = lambda v: lax.ppermute(v, ("yh", "core", "yl"), pairs)
    right_sent = orbital(partner_orbital(1 - yl, core))
    right_first = swap(right_sent)
    right_second = lax.ppermute(right_first, "core", [(0, 1), (1, 0)])

    place = lax.broadcasted_iota(jnp.int32, (16 * PAD, 1), 0)
    dx, dz, r = place // (4 * PAD), (place // PAD) % 4, place % PAD
    chunk = ((x + dx) % 4) * 4 + (z + dz) % 4
    virt = jnp.where(r < ROWS, chunk * ROWS + r, -nvirt)

    def left_rows(first):
        hot = (lax.broadcasted_iota(jnp.int32, (1, nvirt), 1) == virt + first).astype(BF16)
        both = [
            dot(hot, orbital(orbital_order[s]), ((1,), (1,))).astype(BF16).reshape(16, 1, PAD, nq)
            for s in range(NI)
        ]
        return jnp.concatenate(both, axis=1).reshape(16 * NI * PAD, nq)

    target_yh = jnp.where(core == 0, yh, 1 - yh)
    left_own = left_rows(own_a)
    left_sent = left_rows((target_yh * 2 + core) * (nvirt // 4))
    left_other = swap(left_sent)

    right_own = [orbital(partner_orbital(yl, k)) for k in range(KH)]
    right_other = [
        jnp.where(core == 0, right_first, right_second),
        jnp.where(core == 0, right_second, right_first),
    ]

    pair_flat = occ_pair_int.reshape(NI * NI, nq)
    g = [dot(pair_flat, half_ao[t], ((1,), (0,))) for t in range(NI)]
    cell = lambda u, v, t: g[t][u * NI + v]
    fock_terms = []
    for s in range(NI):
        fock_terms.append(2.0 * cell(0, 0, s) - cell(s, 0, 0))
        fock_terms.append(2.0 * (cell(0, 1, s) + cell(1, 0, s)) - cell(s, 1, 0) - cell(s, 0, 1))
        fock_terms.append(2.0 * cell(1, 1, s) - cell(s, 1, 1))
    fock_terms = jnp.stack(fock_terms)
    n_aux = lax.axis_size(AUX)
    tile = half_ao.shape[2] // n_aux
    fock_tile = lax.psum_scatter(
        fock_terms.reshape(6, n_aux, tile).transpose(1, 0, 2), AUX, scatter_dimension=0, tiled=False
    )
    vir_part = jnp.dot(fock_tile, vir_coeff.astype(F32), precision=lax.Precision.HIGHEST)
    share = vir_part.shape[1] // n_aux
    vir_own = lax.psum_scatter(
        vir_part.reshape(6, n_aux, share).transpose(1, 0, 2), AUX, scatter_dimension=0, tiled=False
    )

    pair_other = lax.ppermute(pair_flat, "yl", [(0, 1), (1, 0)])
    z_part = jnp.stack(
        [
            dot(pair_flat, right_own[k], ((1,), (0,))) + dot(pair_other, right_other[k], ((1,), (0,)))
            for k in range(KH)
        ]
    )
    z_sum = lax.psum(z_part, ("x", "z"))

    def by_block(left, swapped):
        blocks = left.reshape(4, 4, NI * PAD, nq)
        blocks = blocks.transpose(1, 0, 2, 3) if swapped else blocks
        return blocks.reshape(4, 2, 2 * NI * PAD, nq)

    summed = []
    for k, (first, second) in enumerate((("x", "z"), ("z", "x"))):
        lo_, oo_ = by_block(left_own, k == 1), by_block(left_other, k == 1)
        v = {}
        for d in (2, 1, 3, 0):
            v[d] = [
                dot(lo_[d, h], right_own[k], ((1,), (0,))) + dot(oo_[d, h], right_other[k], ((1,), (0,)))
                for h in range(2)
            ]
        u = ring_sum(v, first).reshape(4, 2, PAD, nvirt)
        w = ring_sum([[u[d, 0], u[d, 1]] for d in range(4)], second)
        summed.append(w.reshape(NI, PAD, nvirt))

    own_chunk = x * 4 + z
    padded = jnp.concatenate([vir_energy, vir_energy[:2]])
    row_energy = lax.dynamic_slice_in_dim(padded, own_a + own_chunk * ROWS, PAD)
    left_energy = jnp.stack([occ_energy[orbital_order[s]] for s in range(NI)])
    amps = []
    for k in range(KH):
        e_k = lax.dynamic_index_in_dim(occ_energy, partner_orbital(yl, k), 0, keepdims=False)
        denominator = (
            row_energy[None, :, None] + vir_energy[None, None, :] - left_energy[:, None, None] - e_k
        )
        amps.append((-summed[k] / denominator).astype(BF16))

    wide = [a.astype(F32) for a in amps]
    entries = [
        -sum(jnp.sum(w[s] * w[t]) for w in wide) for s, t in ((0, 0), (0, 1), (1, 1))
    ]
    density = lax.psum(jnp.stack(entries), OCC_AUX)
    occ_rows = []
    for s in range(NI):
        row = jnp.zeros((PAD,), F32)
        for k in range(KH):
            for u in range(NI):
                row = row - jnp.sum(wide[k][u] * z_sum[k, u * NI + s][None, :], axis=1)
        occ_rows.append(row)
    occ_rows = jnp.stack(occ_rows)
    mine = lax.dynamic_slice_in_dim(occ_rows, yl * share, share, axis=1)
    theirs = lax.dynamic_slice_in_dim(occ_rows, (1 - yl) * share, share, axis=1)
    occ_side = mine + lax.ppermute(theirs, "yl", [(0, 1), (1, 0)])

    gammas = []
    for k, (first, second) in enumerate((("z", "x"), ("x", "z"))):
        own = jnp.concatenate(ring_gather(amps[k].reshape(NI * PAD, nvirt), first))
        blocks = ring_gather(own, second)
        parts = [
            [dot(b, right[k], ((1,), (1,))) for b in blocks] for right in (right_other, right_own)
        ]
        both = [jnp.concatenate(p).reshape(4, 4, NI * PAD, nq) for p in parts]
        if k == 1:
            both = [b.transpose(1, 0, 2, 3) for b in both]
        gammas.append(both)
    gamma_sent = (gammas[0][0] + gammas[1][0]).astype(BF16)
    gamma_got = lax.ppermute(gamma_sent, "yl", [(0, 1), (1, 0)])
    gamma_rows = (gammas[0][1] + gammas[1][1] + gamma_got.astype(F32)).astype(BF16)
    gamma_rows = gamma_rows.reshape(16, NI, PAD, nq)
    target = lax.broadcasted_iota(jnp.int32, (nvirt // 4, 1), 0)
    back = (target == virt.reshape(1, 16 * PAD)).astype(BF16)
    gamma_out = jnp.stack(
        [
            dot(back, gamma_rows[:, s].reshape(16 * PAD, nq), ((1,), (0,))).astype(BF16)
            for s in range(NI)
        ]
    )
    gamma_out = jnp.transpose(gamma_out, (2, 0, 1))

    weights = vir_own.reshape(NI, 3, share)
    gradient = occ_side + jnp.sum(weights * density[None, :, None], axis=1)
    return (gamma_out, gradient)


def solution(mesh):
    torus = Mesh(mesh.devices.reshape(2, 2, 4, 4, 2), OCC_AUX)
    occ = ("yh", "core")
    return jax.shard_map(
        local,
        mesh=torus,
        in_specs=(
            P(AUX, None, None),
            P(),
            P(),
            P(),
            P(),
            P(None, None, AUX),
            P(None, AUX, None),
            P(AUX, occ),
        ),
        out_specs=(P(AUX, None, occ), P(None, OCC_AUX)),
        check_vma=False,
    )
```

```python
import jax
import jax.numpy as jnp
import numpy as np
from jax import lax
from jax.sharding import Mesh
from jax.sharding import PartitionSpec as P

NI = 2
KH = 2
ROWS = 30
PAD = 32
AUX = ("x", "z", "yl")
OCC_AUX = ("yh", "core", "x", "z", "yl")
F32 = jnp.float32
BF16 = jnp.bfloat16


def ring(n, d):
    return [(i, (i + d) % n) for i in range(n)]


def up(v, axis):
    return lax.ppermute(v, axis, ring(4, 1))


def down(v, axis):
    return lax.ppermute(v, axis, ring(4, -1))


def dot(a, b, dims):
    return lax.dot_general(a, b, (dims, ((), ())), preferred_element_type=F32)


GROUPS = (((2, 0), (1, 1)), ((2, 1), (3, 0)), ((1, 0), (3, 1)), ((0, 0), (0, 1)))
UNITS = [
    (d1, d2, half2)
    for group in GROUPS
    for d1, half1 in group
    for d2, half2 in sum((list(g) for g in GROUPS[2 * half1 : 2 * half1 + 2]), [])
]


def order_matrix(swapped):
    hot = np.zeros((32, 32), np.float32)
    for i, (d1, d2, s) in enumerate(UNITS):
        dx, dz = (d2, d1) if swapped else (d1, d2)
        hot[i, s * 16 + dx * 4 + dz] = 1
    return np.kron(hot, np.eye(PAD, dtype=np.float32))


def ring_sum(going_up, going_down, middle, own, axis):
    half = own.shape[0] // 2
    got_up = up(going_up, axis)
    got_down = down(going_down, axis)
    from_below = up((middle[:half] + got_up[:half].astype(F32)).astype(BF16), axis)
    from_above = down((middle[half:] + got_down[:half].astype(F32)).astype(BF16), axis)
    low = own[:half] + got_down[half:].astype(F32) + from_below.astype(F32)
    high = own[half:] + got_up[half:].astype(F32) + from_above.astype(F32)
    return low, high


def ring_gather(v, axis):
    below = up(v, axis)
    above = down(v, axis)
    half = v.shape[0] // 2
    lo = up(below[:half], axis)
    hi = down(above[half:], axis)
    return [v, above, jnp.concatenate([lo, hi]), below]


def local(
    three_index,
    occ_energy,
    vir_energy,
    batch_table,
    orbital_order,
    occ_pair_int,
    half_ao,
    vir_coeff,
):
    nq, _, nvirt = three_index.shape
    yh, core, x, z, yl = (lax.axis_index(a) for a in OCC_AUX)
    own_a = (yh * 2 + core) * (nvirt // 4)
    n_aux = lax.axis_size(AUX)
    by_orbital = jnp.transpose(three_index, (1, 0, 2))

    def orbital(i):
        return lax.dynamic_index_in_dim(by_orbital, i, 0, keepdims=False)

    def partner_orbital(half, k):
        return lax.dynamic_index_in_dim(batch_table, half * KH + k, 0, keepdims=False)

    pairs = []
    for h in range(2):
        for c in range(2):
            for t in range(2):
                pairs.append((h * 4 + c * 2 + t, (h if c == 0 else 1 - h) * 4 + c * 2 + 1 - t))
    swap = lambda v: lax.ppermute(v, ("yh", "core", "yl"), pairs)
    flip = lambda v: lax.ppermute(v, "yl", [(0, 1), (1, 0)])
    partners = [partner_orbital(yl, core), partner_orbital(yl, 1 - core)]
    right_first = swap(orbital(partner_orbital(1 - yl, core)))

    place = lax.broadcasted_iota(jnp.int32, (16 * PAD, 1), 0)
    dx, dz, r = place // (4 * PAD), (place // PAD) % 4, place % PAD
    chunk = ((x + dx) % 4) * 4 + (z + dz) % 4
    virt = jnp.where(r < ROWS, chunk * ROWS + r, -nvirt)

    def left_rows(first):
        hot = (lax.broadcasted_iota(jnp.int32, (1, nvirt), 1) == virt + first).astype(BF16)
        both = [
            dot(hot, orbital(orbital_order[s]), ((1,), (1,))).astype(BF16) for s in range(NI)
        ]
        return jnp.concatenate(both)

    target_yh = jnp.where(core == 0, yh, 1 - yh)
    left_other = swap(left_rows((target_yh * 2 + core) * (nvirt // 4)))
    left_own = left_rows(own_a)
    right_second = lax.ppermute(right_first, "core", [(0, 1), (1, 0)])
    right_own = [orbital(i) for i in partners]
    right_other = [right_first, right_second]
    pair_flat = occ_pair_int.reshape(NI * NI, nq)
    pair_other = flip(pair_flat)

    lone = jnp.eye(NI, dtype=BF16)
    spread = (pair_flat[:, None, :, None] * lone[None, :, None, :]).reshape(NI**3, nq * NI)
    half_rows = jnp.transpose(half_ao, (1, 0, 2)).reshape(nq * NI, half_ao.shape[2])
    g = dot(spread, half_rows, ((1,), (0,)))
    cell = lambda u, v, t: g[(u * NI + v) * NI + t]
    fock_terms = []
    for s in range(NI):
        fock_terms.append(2.0 * cell(0, 0, s) - cell(s, 0, 0))
        fock_terms.append(2.0 * (cell(0, 1, s) + cell(1, 0, s)) - cell(s, 1, 0) - cell(s, 0, 1))
        fock_terms.append(2.0 * cell(1, 1, s) - cell(s, 1, 1))
    fock_terms = jnp.stack(fock_terms)
    tile = half_ao.shape[2] // n_aux
    fock_tile = jnp.sum(
        lax.all_to_all(
            fock_terms.reshape(6, n_aux, tile).transpose(1, 0, 2), AUX, 0, 0, tiled=True
        ),
        axis=0,
    )
    vir_part = jnp.dot(fock_tile, vir_coeff.astype(F32), precision=lax.Precision.HIGHEST)

    summed = []
    for k, (first, second) in enumerate((("x", "z"), ("z", "x"))):
        order = jnp.asarray(order_matrix(k == 1), BF16)
        lefts = [dot(order, v, ((1,), (0,))).astype(BF16) for v in (left_own, left_other)]
        rows = lefts[0].shape[0] // 4
        v = []
        for i in range(4):
            cut = [left[i * rows : (i + 1) * rows] for left in lefts]
            v.append(
                dot(cut[0], right_own[k], ((1,), (0,))) + dot(cut[1], right_other[k], ((1,), (0,)))
            )
        low, high = ring_sum(v[0].astype(BF16), v[1].astype(BF16), v[2], v[3], first)
        cut = low.shape[0] // 2
        w = ring_sum(
            low[:cut].astype(BF16), low[cut:].astype(BF16), high[:cut], high[cut:], second
        )
        summed.append(jnp.stack(w))

    own_chunk = x * 4 + z
    padded = jnp.concatenate([vir_energy, vir_energy[:2]])
    row_energy = lax.dynamic_slice_in_dim(padded, own_a + own_chunk * ROWS, PAD)
    left_energy = jnp.stack([occ_energy[orbital_order[s]] for s in range(NI)])
    amps = []
    for k in range(KH):
        e_k = lax.dynamic_index_in_dim(occ_energy, partners[k], 0, keepdims=False)
        denominator = (
            row_energy[None, :, None] + vir_energy[None, None, :] - left_energy[:, None, None] - e_k
        )
        amps.append((-summed[k] / denominator).astype(BF16))

    wide = [a.astype(F32) for a in amps]
    density = -jnp.stack(
        [sum(jnp.sum(w[s] * w[t]) for w in wide) for s, t in ((0, 0), (0, 1), (1, 1))]
    )
    density = density + lax.ppermute(density, "core", [(0, 1), (1, 0)])
    density = density + lax.ppermute(density, "yh", [(0, 1), (1, 0)])

    gammas = []
    for k, (first, second) in enumerate((("z", "x"), ("x", "z"))):
        own = jnp.concatenate(ring_gather(amps[k].reshape(NI * PAD, nvirt), first))
        blocks = ring_gather(own, second)
        parts = [
            [dot(b, right[k], ((1,), (1,))) for b in blocks] for right in (right_other, right_own)
        ]
        both = [jnp.concatenate(p).reshape(4, 4, NI * PAD, nq) for p in parts]
        if k == 1:
            both = [b.transpose(1, 0, 2, 3) for b in both]
        gammas.append(both)
    gamma_other = (gammas[0][0] + gammas[1][0]).reshape(16 * NI * PAD, nq).astype(BF16)
    gamma_got = flip(gamma_other)
    gamma_own = (gammas[0][1] + gammas[1][1]).reshape(16 * NI * PAD, nq)

    place = lax.broadcasted_iota(jnp.int32, (16 * NI * PAD, 1), 0)
    dx, dz, r = place // (8 * PAD), (place // (2 * PAD)) % 4, place % PAD
    chunk = ((x + dx) % 4) * 4 + (z + dz) % 4
    virt = jnp.where(r < ROWS, chunk * ROWS + r, -1)
    back = lax.broadcasted_iota(jnp.int32, (1, nvirt // 4), 1) == virt
    half = (lax.broadcasted_iota(jnp.int32, (1, 16 * NI * PAD), 1) // PAD) % NI
    terms = dot(pair_flat, gamma_own.astype(BF16), ((1,), (1,))) + dot(
        pair_other, gamma_other, ((1,), (1,))
    )
    terms = terms.reshape(NI, NI, -1)
    occ_rows = -jnp.where(half == 0, terms[0], terms[1])
    occ_part = jnp.dot(occ_rows, back.astype(F32), precision=lax.Precision.HIGHEST)
    share = nvirt // 4 // n_aux
    sent = jnp.concatenate([occ_part, vir_part]).reshape(NI + 6, n_aux, share).transpose(1, 0, 2)
    density_row = jnp.broadcast_to(jnp.pad(density, (0, share - 3)), (n_aux, 1, share))
    got = jnp.sum(
        lax.all_to_all(jnp.concatenate([sent, density_row], axis=1), AUX, 0, 0, tiled=True), axis=0
    )
    weights = got[NI : NI + 6].reshape(NI, 3, share)
    gradient = got[:NI] + jnp.sum(weights * got[NI + 6, :3][None, :, None], axis=1)

    gamma_rows = (gamma_own + gamma_got.astype(F32)).astype(BF16)
    hot = back.astype(BF16)
    parity = (place // PAD) % NI
    gamma_out = jnp.stack(
        [
            dot(jnp.where(parity == s, hot, 0), gamma_rows, ((0,), (0,))).astype(BF16)
            for s in range(NI)
        ]
    )
    return (jnp.transpose(gamma_out, (2, 0, 1)), gradient)


def solution(mesh):
    torus = Mesh(mesh.devices.reshape(2, 2, 4, 4, 2), OCC_AUX)
    occ = ("yh", "core")
    return jax.shard_map(
        local,
        mesh=torus,
        in_specs=(
            P(AUX, None, None),
            P(),
            P(),
            P(),
            P(),
            P(None, None, AUX),
            P(None, AUX, None),
            P(AUX, occ),
        ),
        out_specs=(P(AUX, None, occ), P(None, OCC_AUX)),
        check_vma=False,
    )
```

```python
import jax
import jax.numpy as jnp
import numpy as np
from jax import lax
from jax.experimental import pallas as pl
from jax.experimental.pallas import tpu as pltpu
from jax.sharding import Mesh
from jax.sharding import PartitionSpec as P

NI = 2
KH = 2
ROWS = 30
PAD = 32
AUX = ("x", "z", "yl")
OCC_AUX = ("yh", "core", "x", "z", "yl")
F32 = jnp.float32
BF16 = jnp.bfloat16


def ring(n, d):
    return [(i, (i + d) % n) for i in range(n)]


def up(v, axis):
    return lax.ppermute(v, axis, ring(4, 1))


def down(v, axis):
    return lax.ppermute(v, axis, ring(4, -1))


def dot(a, b, dims):
    return lax.dot_general(a, b, (dims, ((), ())), preferred_element_type=F32)


GROUPS = (((2, 0), (1, 1)), ((2, 1), (3, 0)), ((1, 0), (3, 1)), ((0, 0), (0, 1)))
UNITS = [
    (d1, d2, half2)
    for group in GROUPS
    for d1, half1 in group
    for d2, half2 in sum((list(g) for g in GROUPS[2 * half1 : 2 * half1 + 2]), [])
]


def ring_finish(got_up, got_down, middle, own, axis):
    half = own.shape[0] // 2
    from_below = up((middle[:half].astype(F32) + got_up[:half].astype(F32)).astype(BF16), axis)
    from_above = down((middle[half:].astype(F32) + got_down[:half].astype(F32)).astype(BF16), axis)
    low = own[:half].astype(F32) + got_down[half:].astype(F32) + from_below.astype(F32)
    high = own[half:].astype(F32) + got_up[half:].astype(F32) + from_above.astype(F32)
    return low, high


def stacked(*parts):
    def kernel(*refs):
        at = 0
        for ref in refs[:-1]:
            refs[-1][at : at + ref.shape[0]] = ref[...]
            at += ref.shape[0]

    rows = sum(p.shape[0] for p in parts)
    vmem = pl.BlockSpec(memory_space=pltpu.VMEM)
    return pl.pallas_call(
        kernel,
        out_shape=jax.ShapeDtypeStruct((rows, *parts[0].shape[1:]), parts[0].dtype),
        in_specs=[vmem] * len(parts),
        out_specs=vmem,
        compiler_params=pltpu.CompilerParams(vmem_limit_bytes=6 << 20),
        cost_estimate=pl.CostEstimate(
            flops=0, bytes_accessed=4 * rows * parts[0].shape[1], transcendentals=0
        ),
    )(*parts)


VMEM = pl.BlockSpec(memory_space=pltpu.VMEM)


def params(mib):
    return pltpu.CompilerParams(vmem_limit_bytes=mib << 20)


YL, CORE, X, Z, FIRST, FIRST_SENT = 12, 13, 14, 15, 16, 17


def cost(flops, nbytes):
    return pl.CostEstimate(flops=int(flops), bytes_accessed=int(nbytes), transcendentals=0)


WIDE = 384


def picked(info, by_orbital, which):
    _, nq, nvirt = by_orbital.shape
    n = len(which)

    def kernel(info_ref, *refs):
        for i in range(n):
            refs[n + i][0:nq] = refs[i][0]
            refs[n + i][nq:] = jnp.zeros((WIDE - nq, nvirt), BF16)

    return pl.pallas_call(
        kernel,
        out_shape=[jax.ShapeDtypeStruct((WIDE, nvirt), BF16)] * n,
        grid_spec=pltpu.PrefetchScalarGridSpec(
            num_scalar_prefetch=1,
            grid=(1,),
            in_specs=[
                pl.BlockSpec((1, nq, nvirt), lambda i, info_ref, f=f: (f(info_ref), 0, 0))
                for f in which
            ],
            out_specs=[pl.BlockSpec((WIDE, nvirt), lambda i, info_ref: (0, 0))] * n,
        ),
        compiler_params=params(6 * n + 2),
        cost_estimate=cost(0, 4 * n * nq * nvirt),
    )(info, *[by_orbital] * n)


def rows_by_rows(a, b):
    return lax.dot_general(a, b, (((1,), (1,)), ((), ())), preferred_element_type=F32)


def left_rows(info, by_orbital, starts, which):
    _, nq, nvirt = by_orbital.shape
    rows = 16 * PAD
    n = len(which)

    def kernel(info_ref, *refs):
        outs = refs[NI + n :]
        place = lax.broadcasted_iota(jnp.int32, (rows, 1), 0)
        r = place & (PAD - 1)
        dx, dz = place >> 7, (place >> 5) & 3
        chunk = ((info_ref[X] + dx) & 3) * 4 + ((info_ref[Z] + dz) & 3)
        column = lax.broadcasted_iota(jnp.int32, (rows, nvirt), 1)
        for out, start in zip(outs, starts):
            virt = jnp.where(r < ROWS, chunk * ROWS + r + info_ref[start], -1)
            hot = jnp.where(column == virt, 1.0, 0.0).astype(BF16)
            out[...] = jnp.zeros(out.shape, BF16)
            for s in range(NI):
                found = rows_by_rows(hot, refs[s][0])
                out[s * rows : (s + 1) * rows, 0:nq] = found.astype(BF16)
        for i in range(n):
            out = outs[len(starts) + i]
            out[0:nq] = refs[NI + i][0]
            out[nq:] = jnp.zeros((WIDE - nq, nvirt), BF16)

    found_by = [lambda i, s=s: i[6 + s] for s in range(NI)] + which
    return pl.pallas_call(
        kernel,
        out_shape=[jax.ShapeDtypeStruct((NI * rows, WIDE), BF16)] * len(starts)
        + [jax.ShapeDtypeStruct((WIDE, nvirt), BF16)] * n,
        grid_spec=pltpu.PrefetchScalarGridSpec(
            num_scalar_prefetch=1,
            grid=(1,),
            in_specs=[
                pl.BlockSpec((1, nq, nvirt), lambda i, info_ref, f=f: (f(info_ref), 0, 0))
                for f in found_by
            ],
            out_specs=[pl.BlockSpec((NI * rows, WIDE), lambda i, info_ref: (0, 0))] * len(starts)
            + [pl.BlockSpec((WIDE, nvirt), lambda i, info_ref: (0, 0))] * n,
        ),
        compiler_params=params(40),
        cost_estimate=cost(4 * nq * nvirt * rows, (6 + 4 * n) * nq * nvirt),
    )(info, *[by_orbital] * (NI + n))


BLOCK, UNIT = 4 * NI * PAD, NI * PAD


def gamma_near(first, second, right):
    def kernel(*refs):
        out = refs[8]
        a = jnp.concatenate([ref[...] for ref in refs[0:3]])
        b = jnp.concatenate([ref[...] for ref in refs[3:6]])
        out[0 : 3 * BLOCK] = rows_by_rows(a, refs[6][...])
        out[3 * BLOCK :] = jnp.zeros((BLOCK, WIDE), F32)
        more = rows_by_rows(b, refs[7][...])
        for i in range(3):
            for j in range(4):
                out[(j * 4 + i) * UNIT : (j * 4 + i + 1) * UNIT] += more[
                    (i * 4 + j) * UNIT : (i * 4 + j + 1) * UNIT
                ]

    return pl.pallas_call(
        kernel,
        out_shape=jax.ShapeDtypeStruct((4 * BLOCK, WIDE), F32),
        in_specs=[VMEM] * 8,
        out_specs=VMEM,
        compiler_params=params(24),
        cost_estimate=cost(2 * 6 * BLOCK * right[0].size, 12 * BLOCK * right[0].shape[1]),
    )(*first, *second, *right)


def gamma_all(near, first, second, right, dtype):
    def kernel(*refs):
        base, out, last = refs[6:]
        a = jnp.concatenate([ref[...] for ref in refs[0:2]])
        b = jnp.concatenate([ref[...] for ref in refs[2:4]])
        mine = rows_by_rows(a, refs[4][...])
        more = rows_by_rows(b, refs[5][...])
        for i in range(4):
            for j in range(4):
                at = (i * 4 + j) * UNIT
                value = base[at : at + UNIT]
                if i == 3:
                    value = value + mine[j * UNIT : (j + 1) * UNIT]
                if j == 3:
                    value = value + more[i * UNIT : (i + 1) * UNIT]
                out[at : at + UNIT] = value.astype(dtype)
                last[at : at + UNIT] = value[:, WIDE - 128 :]

    return pl.pallas_call(
        kernel,
        out_shape=[
            jax.ShapeDtypeStruct((4 * BLOCK, WIDE), dtype),
            jax.ShapeDtypeStruct((4 * BLOCK, 128), F32),
        ],
        in_specs=[VMEM] * 7,
        out_specs=[VMEM] * 2,
        compiler_params=params(16),
        cost_estimate=cost(2 * 2 * BLOCK * right[0].size, 30 * BLOCK * WIDE),
    )(*first, *second, *right, near)


def pair_rows(lefts, rights, swapped):
    nvirt = rights[0].shape[1]

    def kernel(*refs):
        left = refs[8]
        for i, (d1, d2, s) in enumerate(UNITS):
            dx, dz = (d2, d1) if swapped else (d1, d2)
            at = (s * 16 + dx * 4 + dz) * PAD
            for j in range(2):
                left[i * PAD : (i + 1) * PAD, j * WIDE : (j + 1) * WIDE] = refs[j][at : at + PAD]
        right = jnp.concatenate([refs[2][...], refs[3][...]])
        for i in range(4):
            refs[4 + i][...] = jnp.dot(
                left[i * BLOCK : (i + 1) * BLOCK], right, preferred_element_type=F32
            ).astype(BF16)

    return pl.pallas_call(
        kernel,
        out_shape=[jax.ShapeDtypeStruct((BLOCK, nvirt), BF16)] * 4,
        in_specs=[VMEM] * 4,
        out_specs=[VMEM] * 4,
        scratch_shapes=[pltpu.VMEM((4 * BLOCK, 2 * WIDE), BF16)],
        compiler_params=params(20),
        cost_estimate=cost(16 * BLOCK * WIDE * nvirt, 12 * WIDE * nvirt),
    )(*lefts, *rights)


def halves_of(below, above):
    half = below.shape[0] // 2

    def kernel(below_ref, above_ref, low, high):
        low[...] = below_ref[0:half]
        high[...] = above_ref[half:]

    return pl.pallas_call(
        kernel,
        out_shape=[jax.ShapeDtypeStruct((half, below.shape[1]), below.dtype)] * 2,
        in_specs=[VMEM] * 2,
        out_specs=[VMEM] * 2,
        compiler_params=params(4),
        cost_estimate=cost(0, 4 * below.size),
    )(below, above)


def gamma_placed(info, own, got, width, nq):
    rows = own.shape[0]

    def kernel(info_ref, own_ref, got_ref, out_ref):
        total = (own_ref[:, 0:nq] + got_ref[:, 0:nq].astype(F32)).astype(BF16)
        place = lax.broadcasted_iota(jnp.int32, (1, rows), 1)
        i, j, s, r = place >> 8, (place >> 6) & 3, (place >> 5) & 1, place & (PAD - 1)
        chunk = ((info_ref[X] + (i ^ (i >> 1))) & 3) * 4 + ((info_ref[Z] + (j ^ (j >> 1))) & 3)
        target = jnp.where(r < ROWS, s * width + chunk * ROWS + r, -1)
        row = lax.broadcasted_iota(jnp.int32, (NI * width, rows), 0)
        hot = jnp.where(row == target, 1.0, 0.0).astype(BF16)
        out_ref[...] = jnp.dot(hot, total, preferred_element_type=F32).astype(BF16)

    return pl.pallas_call(
        kernel,
        out_shape=jax.ShapeDtypeStruct((NI * width, nq), BF16),
        in_specs=[pl.BlockSpec(memory_space=pltpu.SMEM), VMEM, VMEM],
        out_specs=VMEM,
        compiler_params=params(14),
        cost_estimate=cost(2 * NI * width * rows * nq, 8 * rows * nq),
    )(info, own, got)


def ring_gather(v, axis):
    below = up(v, axis)
    above = down(v, axis)
    low, high = halves_of(below, above)
    return [v, above, below], [up(low, axis), down(high, axis)]


def local(
    three_index,
    occ_energy,
    vir_energy,
    batch_table,
    orbital_order,
    occ_pair_int,
    half_ao,
    vir_coeff,
):
    nq, _, nvirt = three_index.shape
    yh, core, x, z, yl = (lax.axis_index(a) for a in OCC_AUX)
    own_a = (yh * 2 + core) * (nvirt // 4)
    n_aux = lax.axis_size(AUX)
    by_orbital = jnp.transpose(three_index, (1, 0, 2))

    pairs = []
    for straight in range(2):
        pairs.append([])
        for h in range(2):
            for c in range(2):
                for t in range(2):
                    to = h if c == straight else 1 - h
                    pairs[straight].append((h * 4 + c * 2 + t, to * 4 + c * 2 + 1 - t))
    flip = lambda v: lax.ppermute(v, "yl", [(0, 1), (1, 0)])
    target_yh = jnp.where(core == 1, yh, 1 - yh)
    sent_first = (target_yh * 2 + core) * (nvirt // 4)
    tables = jnp.concatenate([batch_table, orbital_order])
    info = jnp.concatenate(
        [tables, jnp.stack([yl, core, x, z, own_a, sent_first]).astype(jnp.int32)]
    )
    [right_sent] = picked(info, by_orbital, [lambda i: i[(1 - i[YL]) * KH + i[CORE]]])
    right_first = lax.ppermute(right_sent, ("yh", "core", "yl"), pairs[0])
    left_sent, left_own, *right_own = left_rows(
        info,
        by_orbital,
        [FIRST_SENT, FIRST],
        [lambda i: i[i[YL] * KH + i[CORE]], lambda i: i[i[YL] * KH + 1 - i[CORE]]],
    )
    left_other = lax.ppermute(left_sent, ("yh", "core", "yl"), pairs[1])
    half_ao, left_own, right_own = lax.optimization_barrier((half_ao, left_own, right_own))
    pair_flat = occ_pair_int.reshape(NI * NI, nq)
    lone = jnp.eye(NI, dtype=BF16)
    spread = (pair_flat[:, None, :, None] * lone[None, :, None, :]).reshape(NI**3, nq * NI)
    half_rows = jnp.transpose(half_ao, (1, 0, 2)).reshape(nq * NI, half_ao.shape[2])
    right_first, half_rows = lax.optimization_barrier((right_first, half_rows))
    g = dot(spread, half_rows, ((1,), (0,)))
    mix = np.zeros((NI, 3, NI, NI, NI), np.float32)
    for s in range(NI):
        for u in range(NI):
            for v in range(NI):
                mix[s, u + v, u, v, s] += 2.0
                mix[s, u + v, s, u, v] -= 1.0
    fock_terms = jnp.dot(mix.reshape(6, NI**3), g, precision=lax.Precision.HIGHEST)
    tile = half_ao.shape[2] // n_aux
    fock_sent = fock_terms.reshape(6, n_aux, tile).transpose(1, 0, 2)
    left_other, fock_sent = lax.optimization_barrier((left_other, fock_sent))
    right_second = lax.ppermute(right_first, "core", [(0, 1), (1, 0)])
    right_other = [right_first, right_second]
    pair_other = flip(pair_flat)

    lefts = [left_own, left_other]
    terms = [list(pair_rows(lefts, [right_own[0], right_other[0]], False))]
    terms[0][0], right_other[1], fock_sent = lax.optimization_barrier(
        (terms[0][0], right_other[1], fock_sent)
    )
    sums = []
    for k in range(KH):
        z_k = dot(pair_flat, right_own[k][:nq], ((1,), (0,)))
        z_k += dot(pair_other, right_other[k][:nq], ((1,), (0,)))
        high = lax.reduce_precision(z_k, 8, 7)
        sums.append(jnp.concatenate([high, z_k - high]).astype(BF16))
    right_sums = [
        lax.dynamic_update_slice(right_other[k], sums[k], (WIDE - 2 * NI * NI, 0)) for k in range(KH)
    ]
    ups, downs = [up(terms[0][0], "x")], [down(terms[0][1], "x")]
    terms.append(list(pair_rows(lefts, [right_own[1], right_other[1]], True)))
    ups.append(up(terms[1][0], "z"))
    downs.append(down(terms[1][1], "z"))
    fock_tile = jnp.sum(lax.all_to_all(fock_sent, AUX, 0, 0, tiled=True), axis=0)
    vir_part = jnp.dot(fock_tile, vir_coeff.astype(F32), precision=lax.Precision.HIGHEST)
    halves = []
    for k, axis in enumerate(("x", "z")):
        halves.append(ring_finish(ups[k], downs[k], *terms[k][2:], axis))
    summed = []
    for k, axis in enumerate(("z", "x")):
        low, high = halves[k]
        cut = low.shape[0] // 2
        low = low.astype(BF16)
        w = ring_finish(up(low[:cut], axis), down(low[cut:], axis), high[:cut], high[cut:], axis)
        summed.append(jnp.stack(w))

    held = jnp.arange(occ_energy.shape[0])

    def taken(values, where):
        return jnp.sum(jnp.where(where, values, 0), axis=-1)

    first = own_a + (x * 4 + z) * ROWS
    row_energy = taken(
        vir_energy, jnp.arange(nvirt)[None, :] == first + jnp.arange(PAD)[:, None]
    )
    left_energy = taken(occ_energy, held[None, :] == orbital_order[:NI, None])
    amps = []
    for k in range(KH):
        partner = taken(batch_table, held == yl * KH + (core if k == 0 else 1 - core))
        e_k = taken(occ_energy, held == partner)
        denominator = (
            row_energy[None, :, None] + vir_energy[None, None, :] - left_energy[:, None, None] - e_k
        )
        amps.append((-summed[k] / denominator).astype(BF16))

    wide = [a.astype(F32) for a in amps]
    density = -jnp.stack(
        [sum(jnp.sum(w[s] * w[t]) for w in wide) for s, t in ((0, 0), (0, 1), (1, 1))]
    )
    blocks = []
    for k, axis in enumerate(("z", "x")):
        near, far = ring_gather(amps[k].reshape(NI * PAD, nvirt), axis)
        blocks.append(stacked(*near, *far))
    density, blocks = lax.optimization_barrier((density, blocks))
    parts = [ring_gather(blocks[0], "x"), ring_gather(blocks[1], "z")]
    near = [p[0] for p in parts]
    far = [p[1] for p in parts]
    gamma_other, terms = gamma_all(gamma_near(*near, right_sums), *far, right_sums, BF16)
    gamma_other, near = lax.optimization_barrier((gamma_other, near))
    gamma_got = flip(gamma_other)
    gamma_own, _ = gamma_all(gamma_near(*near, right_own), *far, right_own, F32)

    place = lax.broadcasted_iota(jnp.int32, (1, 16 * NI * PAD), 1)
    dx, dz, r = place // (8 * PAD), (place // (2 * PAD)) % 4, place % PAD
    dx, dz = dx ^ (dx >> 1), dz ^ (dz >> 1)
    chunk = ((x + dx) % 4) * 4 + (z + dz) % 4
    virt = jnp.where(r < ROWS, chunk * ROWS + r, -1)
    back = lax.broadcasted_iota(jnp.int32, (nvirt // 4, 1), 0) == virt
    terms = terms[:, 128 - 2 * NI * NI :]
    terms = (terms[:, : NI * NI] + terms[:, NI * NI :]).reshape(16, NI, PAD, NI, NI)
    occ_rows = -jnp.stack([terms[:, 0, :, 0], terms[:, 1, :, 1]], axis=1).reshape(-1, NI)
    occ_part = lax.dot_general(
        occ_rows, back.astype(F32), (((0,), (1,)), ((), ())), precision=lax.Precision.HIGHEST
    )
    share = nvirt // 4 // n_aux
    sent = jnp.concatenate([occ_part, vir_part]).reshape(NI + 6, n_aux, share).transpose(1, 0, 2)
    density_row = jnp.broadcast_to(jnp.pad(density, (0, share - 3)), (n_aux, 1, share))
    got = jnp.sum(
        lax.all_to_all(jnp.concatenate([sent, density_row], axis=1), AUX, 0, 0, tiled=True), axis=0
    )
    density = got[NI + 6, :3]
    elsewhere = [
        lax.ppermute(density, ("yh", "core"), [(i, i ^ d) for i in range(4)]) for d in range(1, 4)
    ]
    density = density + elsewhere[0] + elsewhere[1] + elsewhere[2]
    weights = got[NI : NI + 6].reshape(NI, 3, share)
    gradient = got[:NI] + jnp.sum(weights * density[None, :, None], axis=1)

    gamma_out = gamma_placed(info, gamma_own, gamma_got, nvirt // 4, nq).reshape(NI, nvirt // 4, nq)
    return (jnp.transpose(gamma_out, (2, 0, 1)), gradient)


def solution(mesh):
    torus = Mesh(mesh.devices.reshape(2, 2, 4, 4, 2), OCC_AUX)
    occ = ("yh", "core")
    return jax.shard_map(
        local,
        mesh=torus,
        in_specs=(
            P(AUX, None, None),
            P(),
            P(),
            P(),
            P(),
            P(None, None, AUX),
            P(None, AUX, None),
            P(AUX, occ),
        ),
        out_specs=(P(AUX, None, occ), P(None, OCC_AUX)),
        check_vma=False,
    )
```

```python
import jax
import jax.numpy as jnp
import numpy as np
from jax import lax
from jax.experimental import pallas as pl
from jax.experimental.pallas import tpu as pltpu
from jax.sharding import Mesh
from jax.sharding import PartitionSpec as P

NI = 2
KH = 2
ROWS = 30
PAD = 32
AUX = ("x", "z", "yl")
OCC_AUX = ("yh", "core", "x", "z", "yl")
F32 = jnp.float32
BF16 = jnp.bfloat16


def ring(n, d):
    return [(i, (i + d) % n) for i in range(n)]


def up(v, axis):
    return lax.ppermute(v, axis, ring(4, 1))


def down(v, axis):
    return lax.ppermute(v, axis, ring(4, -1))


def dot(a, b, dims):
    return lax.dot_general(a, b, (dims, ((), ())), preferred_element_type=F32)


GROUPS = (((2, 0), (1, 1)), ((2, 1), (3, 0)), ((1, 0), (3, 1)), ((0, 0), (0, 1)))
UNITS = [
    (d1, d2, half2)
    for group in GROUPS
    for d1, half1 in group
    for d2, half2 in sum((list(g) for g in GROUPS[2 * half1 : 2 * half1 + 2]), [])
]


def ring_finish(got_up, got_down, middle, own, axis):
    half = own.shape[0] // 2
    from_below = up((middle[:half].astype(F32) + got_up[:half].astype(F32)).astype(BF16), axis)
    from_above = down((middle[half:].astype(F32) + got_down[:half].astype(F32)).astype(BF16), axis)
    low = own[:half].astype(F32) + got_down[half:].astype(F32) + from_below.astype(F32)
    high = own[half:].astype(F32) + got_up[half:].astype(F32) + from_above.astype(F32)
    return low, high


def stacked(*parts):
    def kernel(*refs):
        at = 0
        for ref in refs[:-1]:
            refs[-1][at : at + ref.shape[0]] = ref[...]
            at += ref.shape[0]

    rows = sum(p.shape[0] for p in parts)
    vmem = pl.BlockSpec(memory_space=pltpu.VMEM)
    return pl.pallas_call(
        kernel,
        out_shape=jax.ShapeDtypeStruct((rows, *parts[0].shape[1:]), parts[0].dtype),
        in_specs=[vmem] * len(parts),
        out_specs=vmem,
        compiler_params=pltpu.CompilerParams(vmem_limit_bytes=6 << 20),
        cost_estimate=pl.CostEstimate(
            flops=0, bytes_accessed=4 * rows * parts[0].shape[1], transcendentals=0
        ),
    )(*parts)


VMEM = pl.BlockSpec(memory_space=pltpu.VMEM)


def params(mib):
    return pltpu.CompilerParams(vmem_limit_bytes=mib << 20)


YL, CORE, X, Z, FIRST, FIRST_SENT = 12, 13, 14, 15, 16, 17


def cost(flops, nbytes):
    return pl.CostEstimate(flops=int(flops), bytes_accessed=int(nbytes), transcendentals=0)


WIDE = 384


def picked(info, by_orbital, which):
    _, nq, nvirt = by_orbital.shape
    n = len(which)

    def kernel(info_ref, *refs):
        for i in range(n):
            refs[n + i][0:nq] = refs[i][0]
            refs[n + i][nq:] = jnp.zeros((WIDE - nq, nvirt), BF16)

    return pl.pallas_call(
        kernel,
        out_shape=[jax.ShapeDtypeStruct((WIDE, nvirt), BF16)] * n,
        grid_spec=pltpu.PrefetchScalarGridSpec(
            num_scalar_prefetch=1,
            grid=(1,),
            in_specs=[
                pl.BlockSpec((1, nq, nvirt), lambda i, info_ref, f=f: (f(info_ref), 0, 0))
                for f in which
            ],
            out_specs=[pl.BlockSpec((WIDE, nvirt), lambda i, info_ref: (0, 0))] * n,
        ),
        compiler_params=params(6 * n + 2),
        cost_estimate=cost(0, 4 * n * nq * nvirt),
    )(info, *[by_orbital] * n)


def rows_by_rows(a, b):
    return lax.dot_general(a, b, (((1,), (1,)), ((), ())), preferred_element_type=F32)


def left_rows(info, by_orbital, starts, which):
    _, nq, nvirt = by_orbital.shape
    rows = 16 * PAD
    n = len(which)

    def kernel(info_ref, *refs):
        outs = refs[NI + n :]
        place = lax.broadcasted_iota(jnp.int32, (rows, 1), 0)
        r = place & (PAD - 1)
        dx, dz = place >> 7, (place >> 5) & 3
        chunk = ((info_ref[X] + dx) & 3) * 4 + ((info_ref[Z] + dz) & 3)
        column = lax.broadcasted_iota(jnp.int32, (rows, nvirt), 1)
        for out, start in zip(outs, starts):
            virt = jnp.where(r < ROWS, chunk * ROWS + r + info_ref[start], -1)
            hot = jnp.where(column == virt, 1.0, 0.0).astype(BF16)
            out[...] = jnp.zeros(out.shape, BF16)
            for s in range(NI):
                found = rows_by_rows(hot, refs[s][0])
                out[s * rows : (s + 1) * rows, 0:nq] = found.astype(BF16)
        for i in range(n):
            out = outs[len(starts) + i]
            out[0:nq] = refs[NI + i][0]
            out[nq:] = jnp.zeros((WIDE - nq, nvirt), BF16)

    found_by = [lambda i, s=s: i[6 + s] for s in range(NI)] + which
    return pl.pallas_call(
        kernel,
        out_shape=[jax.ShapeDtypeStruct((NI * rows, WIDE), BF16)] * len(starts)
        + [jax.ShapeDtypeStruct((WIDE, nvirt), BF16)] * n,
        grid_spec=pltpu.PrefetchScalarGridSpec(
            num_scalar_prefetch=1,
            grid=(1,),
            in_specs=[
                pl.BlockSpec((1, nq, nvirt), lambda i, info_ref, f=f: (f(info_ref), 0, 0))
                for f in found_by
            ],
            out_specs=[pl.BlockSpec((NI * rows, WIDE), lambda i, info_ref: (0, 0))] * len(starts)
            + [pl.BlockSpec((WIDE, nvirt), lambda i, info_ref: (0, 0))] * n,
        ),
        compiler_params=params(40),
        cost_estimate=cost(4 * nq * nvirt * rows, (6 + 4 * n) * nq * nvirt),
    )(info, *[by_orbital] * (NI + n))


BLOCK, UNIT = 4 * NI * PAD, NI * PAD


def gamma_near(first, second, right):
    def kernel(*refs):
        out = refs[8]
        a = jnp.concatenate([ref[...] for ref in refs[0:3]])
        b = jnp.concatenate([ref[...] for ref in refs[3:6]])
        out[0 : 3 * BLOCK] = rows_by_rows(a, refs[6][...])
        out[3 * BLOCK :] = jnp.zeros((BLOCK, WIDE), F32)
        more = rows_by_rows(b, refs[7][...])
        for i in range(3):
            for j in range(4):
                out[(j * 4 + i) * UNIT : (j * 4 + i + 1) * UNIT] += more[
                    (i * 4 + j) * UNIT : (i * 4 + j + 1) * UNIT
                ]

    return pl.pallas_call(
        kernel,
        out_shape=jax.ShapeDtypeStruct((4 * BLOCK, WIDE), F32),
        in_specs=[VMEM] * 8,
        out_specs=VMEM,
        compiler_params=params(24),
        cost_estimate=cost(1000, 1000),
    )(*first, *second, *right)


def gamma_all(near, first, second, right, dtype):
    def kernel(*refs):
        base, out, last = refs[6:]
        a = jnp.concatenate([ref[...] for ref in refs[0:2]])
        b = jnp.concatenate([ref[...] for ref in refs[2:4]])
        mine = rows_by_rows(a, refs[4][...])
        more = rows_by_rows(b, refs[5][...])
        for i in range(4):
            for j in range(4):
                at = (i * 4 + j) * UNIT
                value = base[at : at + UNIT]
                if i == 3:
                    value = value + mine[j * UNIT : (j + 1) * UNIT]
                if j == 3:
                    value = value + more[i * UNIT : (i + 1) * UNIT]
                out[at : at + UNIT] = value.astype(dtype)
                last[at : at + UNIT] = value[:, WIDE - 128 :]

    return pl.pallas_call(
        kernel,
        out_shape=[
            jax.ShapeDtypeStruct((4 * BLOCK, WIDE), dtype),
            jax.ShapeDtypeStruct((4 * BLOCK, 128), F32),
        ],
        in_specs=[VMEM] * 7,
        out_specs=[VMEM] * 2,
        compiler_params=params(16),
        cost_estimate=cost(1000, 1000),
    )(*first, *second, *right, near)


def pair_rows(lefts, rights, swapped):
    nvirt = rights[0].shape[1]

    def kernel(*refs):
        left = refs[8]
        for i, (d1, d2, s) in enumerate(UNITS):
            dx, dz = (d2, d1) if swapped else (d1, d2)
            at = (s * 16 + dx * 4 + dz) * PAD
            for j in range(2):
                left[i * PAD : (i + 1) * PAD, j * WIDE : (j + 1) * WIDE] = refs[j][at : at + PAD]
        right = jnp.concatenate([refs[2][...], refs[3][...]])
        for i in range(4):
            refs[4 + i][...] = jnp.dot(
                left[i * BLOCK : (i + 1) * BLOCK], right, preferred_element_type=F32
            ).astype(BF16)

    return pl.pallas_call(
        kernel,
        out_shape=[jax.ShapeDtypeStruct((BLOCK, nvirt), BF16)] * 4,
        in_specs=[VMEM] * 4,
        out_specs=[VMEM] * 4,
        scratch_shapes=[pltpu.VMEM((4 * BLOCK, 2 * WIDE), BF16)],
        compiler_params=params(20),
        cost_estimate=cost(16 * BLOCK * WIDE * nvirt, 12 * WIDE * nvirt),
    )(*lefts, *rights)


def halves_of(below, above):
    half = below.shape[0] // 2

    def kernel(below_ref, above_ref, low, high):
        low[...] = below_ref[0:half]
        high[...] = above_ref[half:]

    return pl.pallas_call(
        kernel,
        out_shape=[jax.ShapeDtypeStruct((half, below.shape[1]), below.dtype)] * 2,
        in_specs=[VMEM] * 2,
        out_specs=[VMEM] * 2,
        compiler_params=params(4),
        cost_estimate=cost(0, 4 * below.size),
    )(below, above)


def gamma_placed(info, own, got, width, nq):
    rows = own.shape[0]

    def kernel(info_ref, own_ref, got_ref, out_ref):
        total = (own_ref[:, 0:nq] + got_ref[:, 0:nq].astype(F32)).astype(BF16)
        place = lax.broadcasted_iota(jnp.int32, (1, rows), 1)
        i, j, s, r = place >> 8, (place >> 6) & 3, (place >> 5) & 1, place & (PAD - 1)
        chunk = ((info_ref[X] + (i ^ (i >> 1))) & 3) * 4 + ((info_ref[Z] + (j ^ (j >> 1))) & 3)
        target = jnp.where(r < ROWS, s * width + chunk * ROWS + r, -1)
        row = lax.broadcasted_iota(jnp.int32, (NI * width, rows), 0)
        hot = jnp.where(row == target, 1.0, 0.0).astype(BF16)
        out_ref[...] = jnp.dot(hot, total, preferred_element_type=F32).astype(BF16)

    return pl.pallas_call(
        kernel,
        out_shape=jax.ShapeDtypeStruct((NI * width, nq), BF16),
        in_specs=[pl.BlockSpec(memory_space=pltpu.SMEM), VMEM, VMEM],
        out_specs=VMEM,
        compiler_params=params(14),
        cost_estimate=cost(2 * NI * width * rows * nq, 8 * rows * nq),
    )(info, own, got)


def ring_gather(v, axis):
    return ring_forward(v, up(v, axis), down(v, axis), axis)


def ring_forward(v, below, above, axis):
    low, high = halves_of(below, above)
    return [v, above, below], [up(low, axis), down(high, axis)]


def local(
    three_index,
    occ_energy,
    vir_energy,
    batch_table,
    orbital_order,
    occ_pair_int,
    half_ao,
    vir_coeff,
):
    nq, _, nvirt = three_index.shape
    yh, core, x, z, yl = (lax.axis_index(a) for a in OCC_AUX)
    own_a = (yh * 2 + core) * (nvirt // 4)
    n_aux = lax.axis_size(AUX)
    by_orbital = jnp.transpose(three_index, (1, 0, 2))

    pairs = []
    for straight in range(2):
        pairs.append([])
        for h in range(2):
            for c in range(2):
                for t in range(2):
                    to = h if c == straight else 1 - h
                    pairs[straight].append((h * 4 + c * 2 + t, to * 4 + c * 2 + 1 - t))
    flip = lambda v: lax.ppermute(v, "yl", [(0, 1), (1, 0)])
    target_yh = jnp.where(core == 1, yh, 1 - yh)
    sent_first = (target_yh * 2 + core) * (nvirt // 4)
    tables = jnp.concatenate([batch_table, orbital_order])
    info = jnp.concatenate(
        [tables, jnp.stack([yl, core, x, z, own_a, sent_first]).astype(jnp.int32)]
    )
    [right_sent] = picked(info, by_orbital, [lambda i: i[(1 - i[YL]) * KH + i[CORE]]])
    right_first = lax.ppermute(right_sent, ("yh", "core", "yl"), pairs[0])
    left_sent, left_own, *right_own = left_rows(
        info,
        by_orbital,
        [FIRST_SENT, FIRST],
        [lambda i: i[i[YL] * KH + i[CORE]], lambda i: i[i[YL] * KH + 1 - i[CORE]]],
    )
    left_other = lax.ppermute(left_sent, ("yh", "core", "yl"), pairs[1])
    half_ao, left_own, right_own = lax.optimization_barrier((half_ao, left_own, right_own))
    pair_flat = occ_pair_int.reshape(NI * NI, nq)
    lone = jnp.eye(NI, dtype=BF16)
    spread = (pair_flat[:, None, :, None] * lone[None, :, None, :]).reshape(NI**3, nq * NI)
    half_rows = jnp.transpose(half_ao, (1, 0, 2)).reshape(nq * NI, half_ao.shape[2])
    right_first, half_rows = lax.optimization_barrier((right_first, half_rows))
    g = dot(spread, half_rows, ((1,), (0,)))
    mix = np.zeros((NI, 3, NI, NI, NI), np.float32)
    for s in range(NI):
        for u in range(NI):
            for v in range(NI):
                mix[s, u + v, u, v, s] += 2.0
                mix[s, u + v, s, u, v] -= 1.0
    fock_terms = jnp.dot(mix.reshape(6, NI**3), g, precision=lax.Precision.HIGHEST)
    tile = half_ao.shape[2] // n_aux
    fock_sent = fock_terms.reshape(6, n_aux, tile).transpose(1, 0, 2)
    left_other, fock_sent = lax.optimization_barrier((left_other, fock_sent))
    right_second = lax.ppermute(right_first, "core", [(0, 1), (1, 0)])
    right_other = [right_first, right_second]
    pair_other = flip(pair_flat)

    lefts = [left_own, left_other]
    terms = [list(pair_rows(lefts, [right_own[0], right_other[0]], False))]
    terms[0][0], right_other[1] = lax.optimization_barrier((terms[0][0], right_other[1]))
    sums = []
    for k in range(KH):
        z_k = dot(pair_flat, right_own[k][:nq], ((1,), (0,)))
        z_k += dot(pair_other, right_other[k][:nq], ((1,), (0,)))
        high = lax.reduce_precision(z_k, 8, 7)
        sums.append(jnp.concatenate([high, z_k - high]).astype(BF16))
    right_sums = [
        lax.dynamic_update_slice(right_other[k], sums[k], (WIDE - 2 * NI * NI, 0)) for k in range(KH)
    ]
    ups, downs = [up(terms[0][0], "x")], [down(terms[0][1], "x")]
    terms.append(list(pair_rows(lefts, [right_own[1], right_other[1]], True)))
    ups.append(up(terms[1][0], "z"))
    downs.append(down(terms[1][1], "z"))
    ups[0], right_sums, fock_sent = lax.optimization_barrier((ups[0], right_sums, fock_sent))
    fock_tile = jnp.sum(lax.all_to_all(fock_sent, AUX, 0, 0, tiled=True), axis=0)
    halves = []
    for k, axis in enumerate(("x", "z")):
        halves.append(ring_finish(ups[k], downs[k], *terms[k][2:], axis))
    summed = []
    for k, axis in enumerate(("z", "x")):
        low, high = halves[k]
        cut = low.shape[0] // 2
        low = low.astype(BF16)
        w = ring_finish(up(low[:cut], axis), down(low[cut:], axis), high[:cut], high[cut:], axis)
        summed.append(jnp.stack(w))

    summed[0], fock_tile = lax.optimization_barrier((summed[0], fock_tile))
    vir_part = jnp.dot(fock_tile, vir_coeff.astype(F32), precision=lax.Precision.HIGHEST)

    held = jnp.arange(occ_energy.shape[0])

    def taken(values, where):
        return jnp.sum(jnp.where(where, values, 0), axis=-1)

    first = own_a + (x * 4 + z) * ROWS
    row_energy = taken(
        vir_energy, jnp.arange(nvirt)[None, :] == first + jnp.arange(PAD)[:, None]
    )
    left_energy = taken(occ_energy, held[None, :] == orbital_order[:NI, None])
    amps = []
    for k in range(KH):
        partner = taken(batch_table, held == yl * KH + (core if k == 0 else 1 - core))
        e_k = taken(occ_energy, held == partner)
        denominator = (
            row_energy[None, :, None] + vir_energy[None, None, :] - left_energy[:, None, None] - e_k
        )
        amps.append((-summed[k] / denominator).astype(BF16))

    wide = [a.astype(F32) for a in amps]
    density = -jnp.stack(
        [sum(jnp.sum(w[s] * w[t]) for w in wide) for s, t in ((0, 0), (0, 1), (1, 1))]
    )
    blocks = []
    for k, axis in enumerate(("z", "x")):
        near, far = ring_gather(amps[k].reshape(NI * PAD, nvirt), axis)
        blocks.append(stacked(*near, *far))
    density, blocks = lax.optimization_barrier((density, blocks))
    elsewhere = [
        lax.ppermute(density, ("yh", "core"), [(i, i ^ d) for i in range(4)]) for d in range(1, 4)
    ]
    density = density + elsewhere[0] + elsewhere[1] + elsewhere[2]
    parts = []
    for block, axis in zip(blocks, ("x", "z")):
        below, above = up(block, axis), down(block, axis)
        density, below = lax.optimization_barrier((density, below))
        parts.append(ring_forward(block, below, above, axis))
    near = [p[0] for p in parts]
    far = [p[1] for p in parts]
    gamma_other, terms = gamma_all(gamma_near(*near, right_sums), *far, right_sums, BF16)
    gamma_other, near = lax.optimization_barrier((gamma_other, near))
    gamma_got = flip(gamma_other)
    gamma_own, _ = gamma_all(gamma_near(*near, right_own), *far, right_own, F32)

    place = lax.broadcasted_iota(jnp.int32, (1, 16 * NI * PAD), 1)
    dx, dz, r = place // (8 * PAD), (place // (2 * PAD)) % 4, place % PAD
    dx, dz = dx ^ (dx >> 1), dz ^ (dz >> 1)
    chunk = ((x + dx) % 4) * 4 + (z + dz) % 4
    virt = jnp.where(r < ROWS, chunk * ROWS + r, -1)
    back = lax.broadcasted_iota(jnp.int32, (nvirt // 4, 1), 0) == virt
    terms = terms[:, 128 - 2 * NI * NI :]
    terms = (terms[:, : NI * NI] + terms[:, NI * NI :]).reshape(16, NI, PAD, NI, NI)
    occ_rows = -jnp.stack([terms[:, 0, :, 0], terms[:, 1, :, 1]], axis=1).reshape(-1, NI)
    occ_part = lax.dot_general(
        occ_rows, back.astype(F32), (((0,), (1,)), ((), ())), precision=lax.Precision.HIGHEST
    )
    share = nvirt // 4 // n_aux
    sent = jnp.concatenate([occ_part, vir_part]).reshape(NI + 6, n_aux, share).transpose(1, 0, 2)
    density_row = jnp.broadcast_to(jnp.pad(density, (0, share - 3)), (n_aux, 1, share))
    got = jnp.sum(
        lax.all_to_all(jnp.concatenate([sent, density_row], axis=1), AUX, 0, 0, tiled=True), axis=0
    )
    density = got[NI + 6, :3]
    weights = got[NI : NI + 6].reshape(NI, 3, share)
    gradient = got[:NI] + jnp.sum(weights * density[None, :, None], axis=1)

    gamma_out = gamma_placed(info, gamma_own, gamma_got, nvirt // 4, nq).reshape(NI, nvirt // 4, nq)
    return (jnp.transpose(gamma_out, (2, 0, 1)), gradient)


def solution(mesh):
    torus = Mesh(mesh.devices.reshape(2, 2, 4, 4, 2), OCC_AUX)
    occ = ("yh", "core")
    return jax.shard_map(
        local,
        mesh=torus,
        in_specs=(
            P(AUX, None, None),
            P(),
            P(),
            P(),
            P(),
            P(None, None, AUX),
            P(None, AUX, None),
            P(AUX, occ),
        ),
        out_specs=(P(AUX, None, occ), P(None, OCC_AUX)),
        check_vma=False,
    )
```

```python
import jax
import jax.numpy as jnp
import numpy as np
from jax import lax
from jax.experimental import pallas as pl
from jax.experimental.pallas import tpu as pltpu
from jax.sharding import Mesh
from jax.sharding import PartitionSpec as P

NI = 2
KH = 2
ROWS = 30
PAD = 32
AUX = ("x", "z", "yl")
OCC_AUX = ("yh", "core", "x", "z", "yl")
F32 = jnp.float32
BF16 = jnp.bfloat16


def ring(n, d):
    return [(i, (i + d) % n) for i in range(n)]


def up(v, axis):
    return lax.ppermute(v, axis, ring(4, 1))


def down(v, axis):
    return lax.ppermute(v, axis, ring(4, -1))


def dot(a, b, dims):
    return lax.dot_general(a, b, (dims, ((), ())), preferred_element_type=F32)


GROUPS = (((2, 0), (1, 1)), ((2, 1), (3, 0)), ((1, 0), (3, 1)), ((0, 0), (0, 1)))
UNITS = [
    (d1, d2, half2)
    for group in GROUPS
    for d1, half1 in group
    for d2, half2 in sum((list(g) for g in GROUPS[2 * half1 : 2 * half1 + 2]), [])
]


def ring_finish(got_up, got_down, middle, own, axis):
    half = own.shape[0] // 2
    from_below = up((middle[:half].astype(F32) + got_up[:half].astype(F32)).astype(BF16), axis)
    from_above = down((middle[half:].astype(F32) + got_down[:half].astype(F32)).astype(BF16), axis)
    low = own[:half].astype(F32) + got_down[half:].astype(F32) + from_below.astype(F32)
    high = own[half:].astype(F32) + got_up[half:].astype(F32) + from_above.astype(F32)
    return low, high


def stacked(*parts):
    def kernel(*refs):
        at = 0
        for ref in refs[:-1]:
            refs[-1][at : at + ref.shape[0]] = ref[...]
            at += ref.shape[0]

    rows = sum(p.shape[0] for p in parts)
    vmem = pl.BlockSpec(memory_space=pltpu.VMEM)
    return pl.pallas_call(
        kernel,
        out_shape=jax.ShapeDtypeStruct((rows, *parts[0].shape[1:]), parts[0].dtype),
        in_specs=[vmem] * len(parts),
        out_specs=vmem,
        compiler_params=pltpu.CompilerParams(vmem_limit_bytes=6 << 20),
        cost_estimate=pl.CostEstimate(
            flops=0, bytes_accessed=4 * rows * parts[0].shape[1], transcendentals=0
        ),
    )(*parts)


VMEM = pl.BlockSpec(memory_space=pltpu.VMEM)


def params(mib):
    return pltpu.CompilerParams(vmem_limit_bytes=mib << 20)


YL, CORE, X, Z, FIRST, FIRST_SENT = 12, 13, 14, 15, 16, 17


def cost(flops, nbytes):
    return pl.CostEstimate(flops=int(flops), bytes_accessed=int(nbytes), transcendentals=0)


WIDE = 384


def picked(info, by_orbital, which):
    _, nq, nvirt = by_orbital.shape
    n = len(which)

    def kernel(info_ref, *refs):
        for i in range(n):
            refs[n + i][0:nq] = refs[i][0]
            refs[n + i][nq:] = jnp.zeros((WIDE - nq, nvirt), BF16)

    return pl.pallas_call(
        kernel,
        out_shape=[jax.ShapeDtypeStruct((WIDE, nvirt), BF16)] * n,
        grid_spec=pltpu.PrefetchScalarGridSpec(
            num_scalar_prefetch=1,
            grid=(1,),
            in_specs=[
                pl.BlockSpec((1, nq, nvirt), lambda i, info_ref, f=f: (f(info_ref), 0, 0))
                for f in which
            ],
            out_specs=[pl.BlockSpec((WIDE, nvirt), lambda i, info_ref: (0, 0))] * n,
        ),
        compiler_params=params(6 * n + 2),
        cost_estimate=cost(0, 4 * n * nq * nvirt),
    )(info, *[by_orbital] * n)


def rows_by_rows(a, b):
    return lax.dot_general(a, b, (((1,), (1,)), ((), ())), preferred_element_type=F32)


def left_rows(info, by_orbital, starts, which):
    _, nq, nvirt = by_orbital.shape
    rows = 16 * PAD
    n = len(which)

    def kernel(info_ref, *refs):
        outs = refs[NI + n :]
        place = lax.broadcasted_iota(jnp.int32, (rows, 1), 0)
        r = place & (PAD - 1)
        dx, dz = place >> 7, (place >> 5) & 3
        chunk = ((info_ref[X] + dx) & 3) * 4 + ((info_ref[Z] + dz) & 3)
        column = lax.broadcasted_iota(jnp.int32, (rows, nvirt), 1)
        for out, start in zip(outs, starts):
            virt = jnp.where(r < ROWS, chunk * ROWS + r + info_ref[start], -1)
            hot = jnp.where(column == virt, 1.0, 0.0).astype(BF16)
            out[...] = jnp.zeros(out.shape, BF16)
            for s in range(NI):
                found = rows_by_rows(hot, refs[s][0])
                out[s * rows : (s + 1) * rows, 0:nq] = found.astype(BF16)
        for i in range(n):
            out = outs[len(starts) + i]
            out[0:nq] = refs[NI + i][0]
            out[nq:] = jnp.zeros((WIDE - nq, nvirt), BF16)

    found_by = [lambda i, s=s: i[6 + s] for s in range(NI)] + which
    return pl.pallas_call(
        kernel,
        out_shape=[jax.ShapeDtypeStruct((NI * rows, WIDE), BF16)] * len(starts)
        + [jax.ShapeDtypeStruct((WIDE, nvirt), BF16)] * n,
        grid_spec=pltpu.PrefetchScalarGridSpec(
            num_scalar_prefetch=1,
            grid=(1,),
            in_specs=[
                pl.BlockSpec((1, nq, nvirt), lambda i, info_ref, f=f: (f(info_ref), 0, 0))
                for f in found_by
            ],
            out_specs=[pl.BlockSpec((NI * rows, WIDE), lambda i, info_ref: (0, 0))] * len(starts)
            + [pl.BlockSpec((WIDE, nvirt), lambda i, info_ref: (0, 0))] * n,
        ),
        compiler_params=params(40),
        cost_estimate=cost(4 * nq * nvirt * rows, (6 + 4 * n) * nq * nvirt),
    )(info, *[by_orbital] * (NI + n))


BLOCK, UNIT = 4 * NI * PAD, NI * PAD


def gamma_near(first, second, right):
    def kernel(*refs):
        out = refs[8]
        a = jnp.concatenate([ref[...] for ref in refs[0:3]])
        b = jnp.concatenate([ref[...] for ref in refs[3:6]])
        out[0 : 3 * BLOCK] = rows_by_rows(a, refs[6][...])
        out[3 * BLOCK :] = jnp.zeros((BLOCK, WIDE), F32)
        more = rows_by_rows(b, refs[7][...])
        for i in range(3):
            for j in range(4):
                out[(j * 4 + i) * UNIT : (j * 4 + i + 1) * UNIT] += more[
                    (i * 4 + j) * UNIT : (i * 4 + j + 1) * UNIT
                ]

    return pl.pallas_call(
        kernel,
        out_shape=jax.ShapeDtypeStruct((4 * BLOCK, WIDE), F32),
        in_specs=[VMEM] * 8,
        out_specs=VMEM,
        compiler_params=params(24),
        cost_estimate=cost(1000, 1000),
    )(*first, *second, *right)


def gamma_all(near, first, second, right, dtype):
    n = NI * NI

    def kernel(*refs):
        base, out, terms, last = refs[6:]
        a = jnp.concatenate([ref[...] for ref in refs[0:2]])
        b = jnp.concatenate([ref[...] for ref in refs[2:4]])
        mine = rows_by_rows(a, refs[4][...])
        more = rows_by_rows(b, refs[5][...])
        for i in range(4):
            for j in range(4):
                at = (i * 4 + j) * UNIT
                value = base[at : at + UNIT]
                if i == 3:
                    value = value + mine[j * UNIT : (j + 1) * UNIT]
                if j == 3:
                    value = value + more[i * UNIT : (i + 1) * UNIT]
                out[at : at + UNIT] = value.astype(dtype)
                last[at : at + UNIT] = value[:, WIDE - 128 :]
        turned = last[...].T
        terms[...] = turned[128 - 2 * n : 128 - n] + turned[128 - n :]

    return pl.pallas_call(
        kernel,
        out_shape=[
            jax.ShapeDtypeStruct((4 * BLOCK, WIDE), dtype),
            jax.ShapeDtypeStruct((n, 4 * BLOCK), F32),
        ],
        in_specs=[VMEM] * 7,
        out_specs=[VMEM] * 2,
        scratch_shapes=[pltpu.VMEM((4 * BLOCK, 128), F32)],
        compiler_params=params(16),
        cost_estimate=cost(1000, 1000),
    )(*first, *second, *right, near)


def pair_rows(lefts, rights, swapped):
    nvirt = rights[0].shape[1]

    def kernel(*refs):
        left = refs[8]
        for i, (d1, d2, s) in enumerate(UNITS):
            dx, dz = (d2, d1) if swapped else (d1, d2)
            at = (s * 16 + dx * 4 + dz) * PAD
            for j in range(2):
                left[i * PAD : (i + 1) * PAD, j * WIDE : (j + 1) * WIDE] = refs[j][at : at + PAD]
        right = jnp.concatenate([refs[2][...], refs[3][...]])
        for i in range(4):
            refs[4 + i][...] = jnp.dot(
                left[i * BLOCK : (i + 1) * BLOCK], right, preferred_element_type=F32
            ).astype(BF16)

    return pl.pallas_call(
        kernel,
        out_shape=[jax.ShapeDtypeStruct((BLOCK, nvirt), BF16)] * 4,
        in_specs=[VMEM] * 4,
        out_specs=[VMEM] * 4,
        scratch_shapes=[pltpu.VMEM((4 * BLOCK, 2 * WIDE), BF16)],
        compiler_params=params(20),
        cost_estimate=cost(16 * BLOCK * WIDE * nvirt, 12 * WIDE * nvirt),
    )(*lefts, *rights)


def halves_of(below, above):
    half = below.shape[0] // 2

    def kernel(below_ref, above_ref, low, high):
        low[...] = below_ref[0:half]
        high[...] = above_ref[half:]

    return pl.pallas_call(
        kernel,
        out_shape=[jax.ShapeDtypeStruct((half, below.shape[1]), below.dtype)] * 2,
        in_specs=[VMEM] * 2,
        out_specs=[VMEM] * 2,
        compiler_params=params(4),
        cost_estimate=cost(0, 4 * below.size),
    )(below, above)


def gamma_placed(info, own, got, width, nq):
    rows = own.shape[0]

    def kernel(info_ref, own_ref, got_ref, out_ref):
        total = (own_ref[:, 0:nq] + got_ref[:, 0:nq].astype(F32)).astype(BF16)
        place = lax.broadcasted_iota(jnp.int32, (1, rows), 1)
        i, j, s, r = place >> 8, (place >> 6) & 3, (place >> 5) & 1, place & (PAD - 1)
        chunk = ((info_ref[X] + (i ^ (i >> 1))) & 3) * 4 + ((info_ref[Z] + (j ^ (j >> 1))) & 3)
        target = jnp.where(r < ROWS, s * width + chunk * ROWS + r, -1)
        row = lax.broadcasted_iota(jnp.int32, (NI * width, rows), 0)
        hot = jnp.where(row == target, 1.0, 0.0).astype(BF16)
        out_ref[...] = jnp.dot(hot, total, preferred_element_type=F32).astype(BF16)

    return pl.pallas_call(
        kernel,
        out_shape=jax.ShapeDtypeStruct((NI * width, nq), BF16),
        in_specs=[pl.BlockSpec(memory_space=pltpu.SMEM), VMEM, VMEM],
        out_specs=VMEM,
        compiler_params=params(14),
        cost_estimate=cost(2 * NI * width * rows * nq, 8 * rows * nq),
    )(info, own, got)


def ring_gather(v, axis):
    return ring_forward(v, up(v, axis), down(v, axis), axis)


def ring_forward(v, below, above, axis):
    low, high = halves_of(below, above)
    return [v, above, below], [up(low, axis), down(high, axis)]


def local(
    three_index,
    occ_energy,
    vir_energy,
    batch_table,
    orbital_order,
    occ_pair_int,
    half_ao,
    vir_coeff,
):
    nq, _, nvirt = three_index.shape
    yh, core, x, z, yl = (lax.axis_index(a) for a in OCC_AUX)
    own_a = (yh * 2 + core) * (nvirt // 4)
    n_aux = lax.axis_size(AUX)
    by_orbital = jnp.transpose(three_index, (1, 0, 2))

    pairs = []
    for straight in range(2):
        pairs.append([])
        for h in range(2):
            for c in range(2):
                for t in range(2):
                    to = h if c == straight else 1 - h
                    pairs[straight].append((h * 4 + c * 2 + t, to * 4 + c * 2 + 1 - t))
    flip = lambda v: lax.ppermute(v, "yl", [(0, 1), (1, 0)])
    target_yh = jnp.where(core == 1, yh, 1 - yh)
    sent_first = (target_yh * 2 + core) * (nvirt // 4)
    tables = jnp.concatenate([batch_table, orbital_order])
    info = jnp.concatenate(
        [tables, jnp.stack([yl, core, x, z, own_a, sent_first]).astype(jnp.int32)]
    )
    [right_sent] = picked(info, by_orbital, [lambda i: i[(1 - i[YL]) * KH + i[CORE]]])
    right_first = lax.ppermute(right_sent, ("yh", "core", "yl"), pairs[0])
    left_sent, left_own, *right_own = left_rows(
        info,
        by_orbital,
        [FIRST_SENT, FIRST],
        [lambda i: i[i[YL] * KH + i[CORE]], lambda i: i[i[YL] * KH + 1 - i[CORE]]],
    )
    left_other = lax.ppermute(left_sent, ("yh", "core", "yl"), pairs[1])
    half_ao, left_own, right_own = lax.optimization_barrier((half_ao, left_own, right_own))
    pair_flat = occ_pair_int.reshape(NI * NI, nq)
    lone = jnp.eye(NI, dtype=BF16)
    spread = (pair_flat[:, None, :, None] * lone[None, :, None, :]).reshape(NI**3, nq * NI)
    half_rows = jnp.transpose(half_ao, (1, 0, 2)).reshape(nq * NI, half_ao.shape[2])
    right_first, half_rows = lax.optimization_barrier((right_first, half_rows))
    g = dot(spread, half_rows, ((1,), (0,)))
    mix = np.zeros((NI, 3, NI, NI, NI), np.float32)
    for s in range(NI):
        for u in range(NI):
            for v in range(NI):
                mix[s, u + v, u, v, s] += 2.0
                mix[s, u + v, s, u, v] -= 1.0
    fock_terms = jnp.dot(mix.reshape(6, NI**3), g, precision=lax.Precision.HIGHEST)
    tile = half_ao.shape[2] // n_aux
    fock_sent = fock_terms.reshape(6, n_aux, tile).transpose(1, 0, 2)
    left_other, fock_sent = lax.optimization_barrier((left_other, fock_sent))
    right_second = lax.ppermute(right_first, "core", [(0, 1), (1, 0)])
    right_other = [right_first, right_second]
    pair_other = flip(pair_flat)

    lefts = [left_own, left_other]
    terms = [list(pair_rows(lefts, [right_own[0], right_other[0]], False))]
    terms[0][0], right_other[1] = lax.optimization_barrier((terms[0][0], right_other[1]))
    sums = []
    for k in range(KH):
        z_k = dot(pair_flat, right_own[k][:nq], ((1,), (0,)))
        z_k += dot(pair_other, right_other[k][:nq], ((1,), (0,)))
        high = lax.reduce_precision(z_k, 8, 7)
        sums.append(jnp.concatenate([high, z_k - high]).astype(BF16))
    right_sums = [
        lax.dynamic_update_slice(right_other[k], sums[k], (WIDE - 2 * NI * NI, 0)) for k in range(KH)
    ]
    ups, downs = [up(terms[0][0], "x")], [down(terms[0][1], "x")]
    terms.append(list(pair_rows(lefts, [right_own[1], right_other[1]], True)))
    ups.append(up(terms[1][0], "z"))
    downs.append(down(terms[1][1], "z"))
    ups[0], right_sums, fock_sent = lax.optimization_barrier((ups[0], right_sums, fock_sent))
    fock_tile = jnp.sum(lax.all_to_all(fock_sent, AUX, 0, 0, tiled=True), axis=0)
    halves = []
    for k, axis in enumerate(("x", "z")):
        halves.append(ring_finish(ups[k], downs[k], *terms[k][2:], axis))
    summed = []
    for k, axis in enumerate(("z", "x")):
        low, high = halves[k]
        cut = low.shape[0] // 2
        low = low.astype(BF16)
        w = ring_finish(up(low[:cut], axis), down(low[cut:], axis), high[:cut], high[cut:], axis)
        summed.append(jnp.stack(w))

    summed[0], fock_tile = lax.optimization_barrier((summed[0], fock_tile))
    vir_part = jnp.dot(fock_tile, vir_coeff.astype(F32), precision=lax.Precision.HIGHEST)

    held = jnp.arange(occ_energy.shape[0])

    def taken(values, where):
        return jnp.sum(jnp.where(where, values, 0), axis=-1)

    first = own_a + (x * 4 + z) * ROWS
    row_energy = taken(
        vir_energy, jnp.arange(nvirt)[None, :] == first + jnp.arange(PAD)[:, None]
    )
    left_energy = taken(occ_energy, held[None, :] == orbital_order[:NI, None])
    amps = []
    for k in range(KH):
        partner = taken(batch_table, held == yl * KH + (core if k == 0 else 1 - core))
        e_k = taken(occ_energy, held == partner)
        denominator = (
            row_energy[None, :, None] + vir_energy[None, None, :] - left_energy[:, None, None] - e_k
        )
        amps.append((-summed[k] / denominator).astype(BF16))

    wide = [a.astype(F32) for a in amps]
    density = -jnp.stack(
        [sum(jnp.sum(w[s] * w[t]) for w in wide) for s, t in ((0, 0), (0, 1), (1, 1))]
    )
    blocks = []
    for k, axis in enumerate(("z", "x")):
        near, far = ring_gather(amps[k].reshape(NI * PAD, nvirt), axis)
        blocks.append(stacked(*near, *far))
    density, blocks = lax.optimization_barrier((density, blocks))
    elsewhere = [
        lax.ppermute(density, ("yh", "core"), [(i, i ^ d) for i in range(4)]) for d in range(1, 4)
    ]
    density = density + elsewhere[0] + elsewhere[1] + elsewhere[2]
    parts = []
    for block, axis in zip(blocks, ("x", "z")):
        below, above = up(block, axis), down(block, axis)
        density, below = lax.optimization_barrier((density, below))
        parts.append(ring_forward(block, below, above, axis))
    near = [p[0] for p in parts]
    far = [p[1] for p in parts]
    gamma_other, terms = gamma_all(gamma_near(*near, right_sums), *far, right_sums, BF16)
    gamma_other, near = lax.optimization_barrier((gamma_other, near))
    gamma_got = flip(gamma_other)
    gamma_own, _ = gamma_all(gamma_near(*near, right_own), *far, right_own, F32)

    place = lax.broadcasted_iota(jnp.int32, (1, 16 * NI * PAD), 1)
    dx, dz, r = place // (8 * PAD), (place // (2 * PAD)) % 4, place % PAD
    dx, dz = dx ^ (dx >> 1), dz ^ (dz >> 1)
    chunk = ((x + dx) % 4) * 4 + (z + dz) % 4
    virt = jnp.where(r < ROWS, chunk * ROWS + r, -1)
    back = lax.broadcasted_iota(jnp.int32, (nvirt // 4, 1), 0) == virt
    half = (lax.broadcasted_iota(jnp.int32, (1, 16 * NI * PAD), 1) // PAD) % NI
    terms = terms.reshape(NI, NI, -1)
    occ_rows = -jnp.where(half == 0, terms[0], terms[1])
    occ_part = lax.dot_general(
        occ_rows, back.astype(F32), (((1,), (1,)), ((), ())), precision=lax.Precision.HIGHEST
    )
    share = nvirt // 4 // n_aux
    sent = jnp.concatenate([occ_part, vir_part]).reshape(NI + 6, n_aux, share).transpose(1, 0, 2)
    density_row = jnp.broadcast_to(jnp.pad(density, (0, share - 3)), (n_aux, 1, share))
    got = jnp.sum(
        lax.all_to_all(jnp.concatenate([sent, density_row], axis=1), AUX, 0, 0, tiled=True), axis=0
    )
    density = got[NI + 6, :3]
    weights = got[NI : NI + 6].reshape(NI, 3, share)
    gradient = got[:NI] + jnp.sum(weights * density[None, :, None], axis=1)

    gamma_out = gamma_placed(info, gamma_own, gamma_got, nvirt // 4, nq).reshape(NI, nvirt // 4, nq)
    return (jnp.transpose(gamma_out, (2, 0, 1)), gradient)


def solution(mesh):
    torus = Mesh(mesh.devices.reshape(2, 2, 4, 4, 2), OCC_AUX)
    occ = ("yh", "core")
    return jax.shard_map(
        local,
        mesh=torus,
        in_specs=(
            P(AUX, None, None),
            P(),
            P(),
            P(),
            P(),
            P(None, None, AUX),
            P(None, AUX, None),
            P(AUX, occ),
        ),
        out_specs=(P(AUX, None, occ), P(None, OCC_AUX)),
        check_vma=False,
    )
```

```python
import jax
import jax.numpy as jnp
import numpy as np
from jax import lax
from jax.experimental import pallas as pl
from jax.experimental.pallas import tpu as pltpu
from jax.sharding import Mesh
from jax.sharding import PartitionSpec as P

NI = 2
KH = 2
ROWS = 30
PAD = 32
AUX = ("x", "z", "yl")
OCC_AUX = ("yh", "core", "x", "z", "yl")
F32 = jnp.float32
BF16 = jnp.bfloat16


def ring(n, d):
    return [(i, (i + d) % n) for i in range(n)]


def up(v, axis):
    return lax.ppermute(v, axis, ring(4, 1))


def down(v, axis):
    return lax.ppermute(v, axis, ring(4, -1))


def dot(a, b, dims):
    return lax.dot_general(a, b, (dims, ((), ())), preferred_element_type=F32)


GROUPS = (((2, 0), (1, 1)), ((2, 1), (3, 0)), ((1, 0), (3, 1)), ((0, 0), (0, 1)))
UNITS = [
    (d1, d2, half2)
    for group in GROUPS
    for d1, half1 in group
    for d2, half2 in sum((list(g) for g in GROUPS[2 * half1 : 2 * half1 + 2]), [])
]


def ring_finish(got_up, got_down, middle, own, axis):
    half = own.shape[0] // 2
    from_below = up((middle[:half].astype(F32) + got_up[:half].astype(F32)).astype(BF16), axis)
    from_above = down((middle[half:].astype(F32) + got_down[:half].astype(F32)).astype(BF16), axis)
    low = own[:half].astype(F32) + got_down[half:].astype(F32) + from_below.astype(F32)
    high = own[half:].astype(F32) + got_up[half:].astype(F32) + from_above.astype(F32)
    return low, high


def stacked(*parts):
    def kernel(*refs):
        at = 0
        for ref in refs[:-1]:
            refs[-1][at : at + ref.shape[0]] = ref[...]
            at += ref.shape[0]

    rows = sum(p.shape[0] for p in parts)
    vmem = pl.BlockSpec(memory_space=pltpu.VMEM)
    return pl.pallas_call(
        kernel,
        out_shape=jax.ShapeDtypeStruct((rows, *parts[0].shape[1:]), parts[0].dtype),
        in_specs=[vmem] * len(parts),
        out_specs=vmem,
        compiler_params=pltpu.CompilerParams(vmem_limit_bytes=6 << 20),
        cost_estimate=pl.CostEstimate(
            flops=0, bytes_accessed=4 * rows * parts[0].shape[1], transcendentals=0
        ),
    )(*parts)


VMEM = pl.BlockSpec(memory_space=pltpu.VMEM)


def params(mib):
    return pltpu.CompilerParams(vmem_limit_bytes=mib << 20)


YL, CORE, X, Z, FIRST, FIRST_SENT = 12, 13, 14, 15, 16, 17


def cost(flops, nbytes):
    return pl.CostEstimate(flops=int(flops), bytes_accessed=int(nbytes), transcendentals=0)


WIDE = 384


def picked(info, by_orbital, which):
    _, nq, nvirt = by_orbital.shape
    n = len(which)

    def kernel(info_ref, *refs):
        for i in range(n):
            refs[n + i][0:nq] = refs[i][0]
            refs[n + i][nq:] = jnp.zeros((WIDE - nq, nvirt), BF16)

    return pl.pallas_call(
        kernel,
        out_shape=[jax.ShapeDtypeStruct((WIDE, nvirt), BF16)] * n,
        grid_spec=pltpu.PrefetchScalarGridSpec(
            num_scalar_prefetch=1,
            grid=(1,),
            in_specs=[
                pl.BlockSpec((1, nq, nvirt), lambda i, info_ref, f=f: (f(info_ref), 0, 0))
                for f in which
            ],
            out_specs=[pl.BlockSpec((WIDE, nvirt), lambda i, info_ref: (0, 0))] * n,
        ),
        compiler_params=params(6 * n + 2),
        cost_estimate=cost(0, 4 * n * nq * nvirt),
    )(info, *[by_orbital] * n)


def rows_by_rows(a, b):
    return lax.dot_general(a, b, (((1,), (1,)), ((), ())), preferred_element_type=F32)


def left_rows(info, by_orbital, starts, which):
    _, nq, nvirt = by_orbital.shape
    rows = 16 * PAD
    n = len(which)

    def kernel(info_ref, *refs):
        outs = refs[NI + n :]
        place = lax.broadcasted_iota(jnp.int32, (rows, 1), 0)
        r = place & (PAD - 1)
        dx, dz = place >> 7, (place >> 5) & 3
        chunk = ((info_ref[X] + dx) & 3) * 4 + ((info_ref[Z] + dz) & 3)
        column = lax.broadcasted_iota(jnp.int32, (rows, nvirt), 1)
        for out, start in zip(outs, starts):
            virt = jnp.where(r < ROWS, chunk * ROWS + r + info_ref[start], -1)
            hot = jnp.where(column == virt, 1.0, 0.0).astype(BF16)
            out[...] = jnp.zeros(out.shape, BF16)
            for s in range(NI):
                found = rows_by_rows(hot, refs[s][0])
                out[s * rows : (s + 1) * rows, 0:nq] = found.astype(BF16)
        for i in range(n):
            out = outs[len(starts) + i]
            out[0:nq] = refs[NI + i][0]
            out[nq:] = jnp.zeros((WIDE - nq, nvirt), BF16)

    found_by = [lambda i, s=s: i[6 + s] for s in range(NI)] + which
    return pl.pallas_call(
        kernel,
        out_shape=[jax.ShapeDtypeStruct((NI * rows, WIDE), BF16)] * len(starts)
        + [jax.ShapeDtypeStruct((WIDE, nvirt), BF16)] * n,
        grid_spec=pltpu.PrefetchScalarGridSpec(
            num_scalar_prefetch=1,
            grid=(1,),
            in_specs=[
                pl.BlockSpec((1, nq, nvirt), lambda i, info_ref, f=f: (f(info_ref), 0, 0))
                for f in found_by
            ],
            out_specs=[pl.BlockSpec((NI * rows, WIDE), lambda i, info_ref: (0, 0))] * len(starts)
            + [pl.BlockSpec((WIDE, nvirt), lambda i, info_ref: (0, 0))] * n,
        ),
        compiler_params=params(40),
        cost_estimate=cost(4 * nq * nvirt * rows, (6 + 4 * n) * nq * nvirt),
    )(info, *[by_orbital] * (NI + n))


BLOCK, UNIT = 4 * NI * PAD, NI * PAD


def gamma_near(first, second, right):
    def kernel(*refs):
        out = refs[8]
        a = jnp.concatenate([ref[...] for ref in refs[0:3]])
        b = jnp.concatenate([ref[...] for ref in refs[3:6]])
        out[0 : 3 * BLOCK] = rows_by_rows(a, refs[6][...])
        out[3 * BLOCK :] = jnp.zeros((BLOCK, WIDE), F32)
        more = rows_by_rows(b, refs[7][...])
        for i in range(3):
            for j in range(4):
                out[(j * 4 + i) * UNIT : (j * 4 + i + 1) * UNIT] += more[
                    (i * 4 + j) * UNIT : (i * 4 + j + 1) * UNIT
                ]

    return pl.pallas_call(
        kernel,
        out_shape=jax.ShapeDtypeStruct((4 * BLOCK, WIDE), F32),
        in_specs=[VMEM] * 8,
        out_specs=VMEM,
        compiler_params=params(24),
        cost_estimate=cost(1000, 1000),
    )(*first, *second, *right)


def gamma_all(near, first, second, right, dtype):
    n = NI * NI

    def kernel(*refs):
        base, out, terms, last = refs[6:]
        a = jnp.concatenate([ref[...] for ref in refs[0:2]])
        b = jnp.concatenate([ref[...] for ref in refs[2:4]])
        mine = rows_by_rows(a, refs[4][...])
        more = rows_by_rows(b, refs[5][...])
        for i in range(4):
            for j in range(4):
                at = (i * 4 + j) * UNIT
                value = base[at : at + UNIT]
                if i == 3:
                    value = value + mine[j * UNIT : (j + 1) * UNIT]
                if j == 3:
                    value = value + more[i * UNIT : (i + 1) * UNIT]
                out[at : at + UNIT] = value.astype(dtype)
                last[at : at + UNIT] = value[:, WIDE - 128 :]
        turned = last[...].T
        terms[...] = turned[128 - 2 * n : 128 - n] + turned[128 - n :]

    return pl.pallas_call(
        kernel,
        out_shape=[
            jax.ShapeDtypeStruct((4 * BLOCK, WIDE), dtype),
            jax.ShapeDtypeStruct((n, 4 * BLOCK), F32),
        ],
        in_specs=[VMEM] * 7,
        out_specs=[VMEM] * 2,
        scratch_shapes=[pltpu.VMEM((4 * BLOCK, 128), F32)],
        compiler_params=params(16),
        cost_estimate=cost(1000, 1000),
    )(*first, *second, *right, near)


def pair_rows(lefts, rights, swapped):
    nvirt = rights[0].shape[1]

    def kernel(*refs):
        left = refs[8]
        for i, (d1, d2, s) in enumerate(UNITS):
            dx, dz = (d2, d1) if swapped else (d1, d2)
            at = (s * 16 + dx * 4 + dz) * PAD
            for j in range(2):
                left[i * PAD : (i + 1) * PAD, j * WIDE : (j + 1) * WIDE] = refs[j][at : at + PAD]
        right = jnp.concatenate([refs[2][...], refs[3][...]])
        for i in range(4):
            refs[4 + i][...] = jnp.dot(
                left[i * BLOCK : (i + 1) * BLOCK], right, preferred_element_type=F32
            ).astype(BF16)

    return pl.pallas_call(
        kernel,
        out_shape=[jax.ShapeDtypeStruct((BLOCK, nvirt), BF16)] * 4,
        in_specs=[VMEM] * 4,
        out_specs=[VMEM] * 4,
        scratch_shapes=[pltpu.VMEM((4 * BLOCK, 2 * WIDE), BF16)],
        compiler_params=params(20),
        cost_estimate=cost(16 * BLOCK * WIDE * nvirt, 12 * WIDE * nvirt),
    )(*lefts, *rights)


def halves_of(below, above):
    half = below.shape[0] // 2

    def kernel(below_ref, above_ref, low, high):
        low[...] = below_ref[0:half]
        high[...] = above_ref[half:]

    return pl.pallas_call(
        kernel,
        out_shape=[jax.ShapeDtypeStruct((half, below.shape[1]), below.dtype)] * 2,
        in_specs=[VMEM] * 2,
        out_specs=[VMEM] * 2,
        compiler_params=params(4),
        cost_estimate=cost(0, 4 * below.size),
    )(below, above)


def gamma_placed(info, own, got, width, nq):
    rows = own.shape[0]

    def kernel(info_ref, own_ref, got_ref, out_ref):
        total = (own_ref[:, 0:nq] + got_ref[:, 0:nq].astype(F32)).astype(BF16)
        place = lax.broadcasted_iota(jnp.int32, (1, rows), 1)
        i, j, s, r = place >> 8, (place >> 6) & 3, (place >> 5) & 1, place & (PAD - 1)
        chunk = ((info_ref[X] + (i ^ (i >> 1))) & 3) * 4 + ((info_ref[Z] + (j ^ (j >> 1))) & 3)
        target = jnp.where(r < ROWS, s * width + chunk * ROWS + r, -1)
        row = lax.broadcasted_iota(jnp.int32, (NI * width, rows), 0)
        hot = jnp.where(row == target, 1.0, 0.0).astype(BF16)
        out_ref[...] = jnp.dot(hot, total, preferred_element_type=F32).astype(BF16)

    return pl.pallas_call(
        kernel,
        out_shape=jax.ShapeDtypeStruct((NI * width, nq), BF16),
        in_specs=[pl.BlockSpec(memory_space=pltpu.SMEM), VMEM, VMEM],
        out_specs=VMEM,
        compiler_params=params(14),
        cost_estimate=cost(2 * NI * width * rows * nq, 8 * rows * nq),
    )(info, own, got)


def ring_gather(v, axis):
    return ring_forward(v, up(v, axis), down(v, axis), axis)


def ring_forward(v, below, above, axis):
    low, high = halves_of(below, above)
    return [v, above, below], [up(low, axis), down(high, axis)]


def local(
    three_index,
    occ_energy,
    vir_energy,
    batch_table,
    orbital_order,
    occ_pair_int,
    half_ao,
    vir_coeff,
):
    nq, _, nvirt = three_index.shape
    yh, core, x, z, yl = (lax.axis_index(a) for a in OCC_AUX)
    own_a = (yh * 2 + core) * (nvirt // 4)
    n_aux = lax.axis_size(AUX)
    by_orbital = jnp.transpose(three_index, (1, 0, 2))

    pairs = []
    for straight in range(2):
        pairs.append([])
        for h in range(2):
            for c in range(2):
                for t in range(2):
                    to = h if c == straight else 1 - h
                    pairs[straight].append((h * 4 + c * 2 + t, to * 4 + c * 2 + 1 - t))
    flip = lambda v: lax.ppermute(v, "yl", [(0, 1), (1, 0)])
    target_yh = jnp.where(core == 1, yh, 1 - yh)
    sent_first = (target_yh * 2 + core) * (nvirt // 4)
    tables = jnp.concatenate([batch_table, orbital_order])
    info = jnp.concatenate(
        [tables, jnp.stack([yl, core, x, z, own_a, sent_first]).astype(jnp.int32)]
    )
    [right_sent] = picked(info, by_orbital, [lambda i: i[(1 - i[YL]) * KH + i[CORE]]])
    right_first = lax.ppermute(right_sent, ("yh", "core", "yl"), pairs[0])
    left_sent, left_own, *right_own = left_rows(
        info,
        by_orbital,
        [FIRST_SENT, FIRST],
        [lambda i: i[i[YL] * KH + i[CORE]], lambda i: i[i[YL] * KH + 1 - i[CORE]]],
    )
    left_other = lax.ppermute(left_sent, ("yh", "core", "yl"), pairs[1])
    half_ao, left_own, right_own = lax.optimization_barrier((half_ao, left_own, right_own))
    pair_flat = occ_pair_int.reshape(NI * NI, nq)
    lone = jnp.eye(NI, dtype=BF16)
    spread = (pair_flat[:, None, :, None] * lone[None, :, None, :]).reshape(NI**3, nq * NI)
    half_rows = jnp.transpose(half_ao, (1, 0, 2)).reshape(nq * NI, half_ao.shape[2])
    right_first, half_rows = lax.optimization_barrier((right_first, half_rows))
    left_other, half_rows = lax.optimization_barrier((left_other, half_rows))
    right_second = lax.ppermute(right_first, "core", [(0, 1), (1, 0)])
    right_other = [right_first, right_second]
    pair_other = flip(pair_flat)

    lefts = [left_own, left_other]
    terms = [list(pair_rows(lefts, [right_own[0], right_other[0]], False))]
    terms[0][0], right_other[1], half_rows = lax.optimization_barrier(
        (terms[0][0], right_other[1], half_rows)
    )
    g = dot(spread, half_rows, ((1,), (0,)))
    mix = np.zeros((NI, 3, NI, NI, NI), np.float32)
    for s in range(NI):
        for u in range(NI):
            for v in range(NI):
                mix[s, u + v, u, v, s] += 2.0
                mix[s, u + v, s, u, v] -= 1.0
    fock_terms = jnp.dot(mix.reshape(6, NI**3), g, precision=lax.Precision.HIGHEST)
    tile = half_ao.shape[2] // n_aux
    fock_sent = fock_terms.reshape(6, n_aux, tile).transpose(1, 0, 2)
    sums = []
    for k in range(KH):
        z_k = dot(pair_flat, right_own[k][:nq], ((1,), (0,)))
        z_k += dot(pair_other, right_other[k][:nq], ((1,), (0,)))
        high = lax.reduce_precision(z_k, 8, 7)
        sums.append(jnp.concatenate([high, z_k - high]).astype(BF16))
    right_sums = [
        lax.dynamic_update_slice(right_other[k], sums[k], (WIDE - 2 * NI * NI, 0)) for k in range(KH)
    ]
    ups, downs = [up(terms[0][0], "x")], [down(terms[0][1], "x")]
    terms.append(list(pair_rows(lefts, [right_own[1], right_other[1]], True)))
    ups.append(up(terms[1][0], "z"))
    downs.append(down(terms[1][1], "z"))
    ups[0], right_sums, fock_sent = lax.optimization_barrier((ups[0], right_sums, fock_sent))
    fock_tile = jnp.sum(lax.all_to_all(fock_sent, AUX, 0, 0, tiled=True), axis=0)
    halves = []
    for k, axis in enumerate(("x", "z")):
        halves.append(ring_finish(ups[k], downs[k], *terms[k][2:], axis))
    summed = []
    for k, axis in enumerate(("z", "x")):
        low, high = halves[k]
        cut = low.shape[0] // 2
        low = low.astype(BF16)
        w = ring_finish(up(low[:cut], axis), down(low[cut:], axis), high[:cut], high[cut:], axis)
        summed.append(jnp.stack(w))

    summed[0], fock_tile = lax.optimization_barrier((summed[0], fock_tile))
    vir_part = jnp.dot(fock_tile, vir_coeff.astype(F32), precision=lax.Precision.HIGHEST)

    held = jnp.arange(occ_energy.shape[0])

    def taken(values, where):
        return jnp.sum(jnp.where(where, values, 0), axis=-1)

    first = own_a + (x * 4 + z) * ROWS
    row_energy = taken(
        vir_energy, jnp.arange(nvirt)[None, :] == first + jnp.arange(PAD)[:, None]
    )
    left_energy = taken(occ_energy, held[None, :] == orbital_order[:NI, None])
    amps = []
    for k in range(KH):
        partner = taken(batch_table, held == yl * KH + (core if k == 0 else 1 - core))
        e_k = taken(occ_energy, held == partner)
        denominator = (
            row_energy[None, :, None] + vir_energy[None, None, :] - left_energy[:, None, None] - e_k
        )
        amps.append((-summed[k] / denominator).astype(BF16))

    wide = [a.astype(F32) for a in amps]
    density = -jnp.stack(
        [sum(jnp.sum(w[s] * w[t]) for w in wide) for s, t in ((0, 0), (0, 1), (1, 1))]
    )
    blocks = []
    for k, axis in enumerate(("z", "x")):
        near, far = ring_gather(amps[k].reshape(NI * PAD, nvirt), axis)
        blocks.append(stacked(*near, *far))
    density, blocks = lax.optimization_barrier((density, blocks))
    elsewhere = [
        lax.ppermute(density, ("yh", "core"), [(i, i ^ d) for i in range(4)]) for d in range(1, 4)
    ]
    density = density + elsewhere[0] + elsewhere[1] + elsewhere[2]
    parts = []
    for block, axis in zip(blocks, ("x", "z")):
        below, above = up(block, axis), down(block, axis)
        density, below = lax.optimization_barrier((density, below))
        parts.append(ring_forward(block, below, above, axis))
    near = [p[0] for p in parts]
    far = [p[1] for p in parts]
    gamma_other, terms = gamma_all(gamma_near(*near, right_sums), *far, right_sums, BF16)
    gamma_other, near = lax.optimization_barrier((gamma_other, near))
    gamma_got = flip(gamma_other)
    gamma_own, _ = gamma_all(gamma_near(*near, right_own), *far, right_own, F32)

    place = lax.broadcasted_iota(jnp.int32, (1, 16 * NI * PAD), 1)
    dx, dz, r = place // (8 * PAD), (place // (2 * PAD)) % 4, place % PAD
    dx, dz = dx ^ (dx >> 1), dz ^ (dz >> 1)
    chunk = ((x + dx) % 4) * 4 + (z + dz) % 4
    virt = jnp.where(r < ROWS, chunk * ROWS + r, -1)
    back = lax.broadcasted_iota(jnp.int32, (nvirt // 4, 1), 0) == virt
    half = (lax.broadcasted_iota(jnp.int32, (1, 16 * NI * PAD), 1) // PAD) % NI
    terms = terms.reshape(NI, NI, -1)
    occ_rows = -jnp.where(half == 0, terms[0], terms[1])
    occ_part = lax.dot_general(
        occ_rows, back.astype(F32), (((1,), (1,)), ((), ())), precision=lax.Precision.HIGHEST
    )
    share = nvirt // 4 // n_aux
    sent = jnp.concatenate([occ_part, vir_part]).reshape(NI + 6, n_aux, share).transpose(1, 0, 2)
    density_row = jnp.broadcast_to(jnp.pad(density, (0, share - 3)), (n_aux, 1, share))
    got = jnp.sum(
        lax.all_to_all(jnp.concatenate([sent, density_row], axis=1), AUX, 0, 0, tiled=True), axis=0
    )
    density = got[NI + 6, :3]
    weights = got[NI : NI + 6].reshape(NI, 3, share)
    gradient = got[:NI] + jnp.sum(weights * density[None, :, None], axis=1)

    gamma_out = gamma_placed(info, gamma_own, gamma_got, nvirt // 4, nq).reshape(NI, nvirt // 4, nq)
    return (jnp.transpose(gamma_out, (2, 0, 1)), gradient)


def solution(mesh):
    torus = Mesh(mesh.devices.reshape(2, 2, 4, 4, 2), OCC_AUX)
    occ = ("yh", "core")
    return jax.shard_map(
        local,
        mesh=torus,
        in_specs=(
            P(AUX, None, None),
            P(),
            P(),
            P(),
            P(),
            P(None, None, AUX),
            P(None, AUX, None),
            P(AUX, occ),
        ),
        out_specs=(P(AUX, None, occ), P(None, OCC_AUX)),
        check_vma=False,
    )
```
